128 devices in a mesh: row: 8 (over x, core), col: 16 (over z, y).
Axes of the slice: x: 4, y: 4, z: 4, core: 2. Of those that a mesh axis runs over, the one named last changes fastest.
Arguments:
- object_field: float32 [2, 10240, 10240], P(None, 'row', 'col'), may hold values from -6 to 6
- illumination: float32 [2, 256, 256], replicated, may hold values from -6 to 6
- measured: float32 [1536, 256, 256], P(('row', 'col')), may hold values from 0.05 to 5
- offsets: int32 [1536, 2], P(('row', 'col')), may hold values from 0 to 1279, as said below
- counts: int32 [128], P(('row', 'col')), may hold values from 1 to 12, as said below
Outputs:
- new_object: float32 [2, 10240, 10240], P(None, 'row', 'col')
- new_lighting: float32 [2, 256, 256], replicated
The draws below stay inside these ranges and needn't reach their ends.
Inputs may be any that keep to these rules, and one draw needn't show every extreme that they name: `offsets`: first column: row within the tile, below 1280; second column: column within the tile, below 640. `counts`: some tile has all 12 slots live; loads differ strongly between tiles.
All inputs are finite; a program needn't handle non-finite values.
Results may differ from the reference program's by a relative error of at most 0.00021.
Values sent between devices are 32-bit elements; how exact they have to be, the bound alone decides.
A program may use at most 256 MiB of HBM per device.

```python
import math
import jax
import jax.numpy as jnp
from jax import lax

W = 256
TR = 1280
TC = 640
TILE_PATTERN_MAX = 12
ITERS = 2
NDEV = 128
NX = 10240
NY = 10240
PATS = 1536
N_COL = 16


def draw_offsets(key, part):
    key = jax.random.fold_in(key, 7)
    first_key, second_key = jax.random.split(key)
    row_part = jax.random.randint(first_key, (PATS,), 0, TR, dtype=jnp.int32)
    col_part = jax.random.randint(second_key, (PATS,), 0, TC, dtype=jnp.int32)
    table = jnp.stack([row_part, col_part], axis=1)
    table = table.at[0].set(jnp.array([TR - 1, TC - 1], jnp.int32))
    return table.at[1].set(jnp.zeros((2,), jnp.int32))


def draw_counts(key, part):
    key = jax.random.fold_in(key, 5)
    light_key, heavy_key, pick_key, top_key = jax.random.split(key, 4)
    lighter = jax.random.randint(light_key, (NDEV,), 1, TILE_PATTERN_MAX // 2 + 1, dtype=jnp.int32)
    heavier = jax.random.randint(heavy_key, (NDEV,), (TILE_PATTERN_MAX + 1) // 2, TILE_PATTERN_MAX + 1, dtype=jnp.int32)
    picked = jax.random.randint(pick_key, (NDEV,), 0, 4, dtype=jnp.int32) == 0
    loads = jnp.where(picked, heavier, lighter)
    busiest = jax.random.randint(top_key, (), 0, NDEV, dtype=jnp.int32)
    return loads.at[busiest].set(jnp.int32(TILE_PATTERN_MAX))


def levels(own_key, shape, cuts, least, top_value):
    def one(dim, parts):
        steps = jax.random.uniform(jax.random.fold_in(jax.random.fold_in(own_key, 6), dim), (parts,), jnp.float32, least / len(cuts), top_value / len(cuts))
        return jnp.repeat(jnp.exp(steps), shape[dim] // parts).reshape((-1,) + (1,) * (len(shape) - dim - 1))

    gain = one(*cuts[0])
    for cut in cuts[1:]:
        gain = gain * one(*cut)
    return gain


def gaussian(stream_key, extent, width, most, shards=(), held_as=jnp.bfloat16):
    result = jax.random.normal(stream_key, extent, jnp.float32) * width
    if len(shards) > 0:
        result = levels(stream_key, extent, shards, -0.22, 0.18) * result
    return jnp.clip(result, min=-most, max=most).astype(held_as)


def setup_inputs(seed: int = 0) -> dict:
    keys = jax.random.split(jax.random.key(seed), 6)
    return {
        "object_field": gaussian(keys[0], (2, NX, NY), 1.0, 6.0, ((1, 8), (2, 16)), jnp.float32),
        "illumination": gaussian(keys[1], (2, W, W), 1.0, 6.0, (), jnp.float32),
        "measured": jnp.clip(jnp.exp(math.log(5.0) - 4.6051702 * jax.random.uniform(keys[2], (PATS, W, W), jnp.float32) ** levels(keys[2], (PATS, W, W), ((0, 128),), -0.2, 0.2)), 0.05, 5.0),
        "offsets": draw_offsets(jax.random.fold_in(keys[5], 71), 0),
        "counts": draw_counts(jax.random.fold_in(keys[5], 71), 0),
    }


OBJECT_RATE = 0.01
LIGHT_RATE = 0.02

def tables(length):
    counter = jnp.arange(length, dtype=jnp.int32)
    phases = counter[:, None] * counter[None, :] % length
    angles = phases.astype(jnp.float32) * (2.0 * math.pi / length)
    factor = 1.0 / math.sqrt(length)
    return (jnp.cos(angles) * factor, -jnp.sin(angles) * factor)

def product(left_side, right_side):
    return jnp.dot(left_side, right_side, precision=lax.Precision.HIGHEST)

def transform(real_part, imag_part, cos_table, sin_table):
    first_re = product(cos_table, real_part) - product(sin_table, imag_part)
    first_im = product(cos_table, imag_part) + product(sin_table, real_part)
    second_re = product(first_re, cos_table) - product(first_im, sin_table)
    second_im = product(first_re, sin_table) + product(first_im, cos_table)
    return (second_re, second_im)

def pattern_terms(lighting, window, intensity, cos_table, sin_table):
    exit_re = lighting[0] * window[0] - lighting[1] * window[1]
    exit_im = lighting[0] * window[1] + lighting[1] * window[0]
    far_re, far_im = transform(exit_re, exit_im, cos_table, sin_table)
    misfit = far_re * far_re + far_im * far_im - intensity
    back_re, back_im = transform(misfit * far_re, misfit * far_im, cos_table, -sin_table)
    object_term = jnp.stack([lighting[0] * back_re + lighting[1] * back_im, lighting[0] * back_im - lighting[1] * back_re])
    light_term = jnp.stack([window[0] * back_re + window[1] * back_im, window[0] * back_im - window[1] * back_re])
    return (object_term, light_term)

def reference(object_field, illumination, measured, offsets, counts):
    half_width = W // 2
    cos_table, sin_table = tables(W)
    sequential_pass = jnp.arange(PATS, dtype=jnp.int32)
    owning_tiles = sequential_pass // TILE_PATTERN_MAX
    active_flags = (sequential_pass % TILE_PATTERN_MAX < counts[owning_tiles]).astype(jnp.float32)
    row_begin = owning_tiles // N_COL * TR + offsets[:, 0]
    column_begin = owning_tiles % N_COL * TC + offsets[:, 1]
    anchor = jnp.zeros((), jnp.int32)
    light_rate = LIGHT_RATE / PATS
    for sweep in range(ITERS):
        padded = jnp.pad(object_field, ((0, 0), (half_width, half_width), (half_width, half_width)))
        lighting = illumination

        def visit_pattern(totals, element):
            gradient_field, probe_power_sum = totals
            row_at, col_at, intensity, weight = element
            window = lax.dynamic_slice(padded, (anchor, row_at, col_at), (2, W, W))
            object_term, light_term = pattern_terms(lighting, window, intensity, cos_table, sin_table)
            current = lax.dynamic_slice(gradient_field, (anchor, row_at, col_at), (2, W, W))
            gradient_field = lax.dynamic_update_slice(gradient_field, current + weight * object_term, (anchor, row_at, col_at))
            return ((gradient_field, probe_power_sum + weight * light_term), None)
        starting_guess = (jnp.zeros_like(padded), jnp.zeros_like(illumination))
        (gradient_field, probe_power_sum), vacant_slots = lax.scan(visit_pattern, starting_guess, (row_begin, column_begin, measured, active_flags))
        object_field = object_field - OBJECT_RATE * gradient_field[:, half_width:half_width + NX, half_width:half_width + NY]
        illumination = illumination - light_rate * probe_power_sum
    return (object_field, illumination)
```

```python
import math

import jax
import jax.numpy as jnp
import numpy as np
from jax import lax
from jax.experimental import pallas as pl
from jax.experimental.pallas import tpu as pltpu
from jax.sharding import PartitionSpec as P

ITERS = 2
OBJECT_RATE = 0.01
LIGHT_RATE = 0.02
MESH = pl.DeviceIdType.MESH
F32 = jnp.float32
BF16 = jnp.bfloat16
VMEM_LIMIT = 56 * 1024 * 1024


def halves(array):
    high = array.astype(BF16)
    low = (array - high.astype(F32)).astype(BF16)
    return high, low


def factor_tables(length):
    half = length // 2
    index = np.arange(half)
    found = []
    for parity in (0, 1):
        phase = ((2 * index[:, None] + parity) * index[None, :]) % length
        angle = phase * (2.0 * math.pi / length)
        real = np.cos(angle) / math.sqrt(length)
        imag = -np.sin(angle) / math.sqrt(length)
        whole = np.block([[real, -imag], [imag, real]])
        for matrix in (whole, whole.T):
            matrix = matrix.astype(np.float32)
            high = matrix.astype(jnp.bfloat16)
            low = (matrix - high.astype(np.float32)).astype(jnp.bfloat16)
            found.append(np.stack([high, low]))
    return np.stack(found)


def parity_order(length):
    half = length // 2
    order = np.zeros((length, length), np.float32)
    order[2 * np.arange(half), np.arange(half)] = 1
    order[2 * np.arange(half) + 1, half + np.arange(half)] = 1
    return order.astype(jnp.bfloat16)


def dot(left, right):
    return jnp.dot(left, right, preferred_element_type=F32)


def order_kernel(count_ref, order_ref, measured_ref, out_ref, rows_ref):
    slot = pl.program_id(0)

    @pl.when(slot < count_ref[0])
    def _():
        half = rows_ref.shape[2]
        for side in (0, 1):
            rows_ref[side] = measured_ref[0, :, side * half : (side + 1) * half]
        order = order_ref[...]
        for parity in (0, 1):
            picked = pl.ds(parity, half, stride=2)
            block = jnp.concatenate([rows_ref[0, picked, :], rows_ref[1, picked, :]], axis=1)
            high, low = halves(block)
            out_ref[0, parity * half : (parity + 1) * half, :] = dot(high, order) + dot(low, order)


def reorder(measured, counts):
    slots, width, _ = measured.shape
    half = width // 2

    def block(slot, count):
        return (jnp.minimum(slot, count[0] - 1), 0, 0)

    return pl.pallas_call(
        order_kernel,
        grid_spec=pltpu.PrefetchScalarGridSpec(
            num_scalar_prefetch=1,
            grid=(slots,),
            in_specs=[
                pl.BlockSpec((width, width), lambda slot, count: (0, 0)),
                pl.BlockSpec((1, width, width), block),
            ],
            out_specs=pl.BlockSpec((1, width, width), block),
            scratch_shapes=[pltpu.VMEM((2, width, half), F32)],
        ),
        out_shape=jax.ShapeDtypeStruct(measured.shape, F32),
        name="reorder",
    )(counts, jnp.asarray(parity_order(width)), measured)


CHUNK = 32


def patterns_kernel(
    count_ref,
    offset_ref,
    table_ref,
    probe_ref,
    measured_hbm,
    tile_hbm,
    top_hbm,
    bottom_hbm,
    left_hbm,
    right_hbm,
    grad_hbm,
    light_ref,
    ext,
    grad,
    measured_ref,
    probe_rot,
    win,
    op_high,
    op_low,
    res,
    res2,
    in_sems,
    out_sem,
):
    width = probe_ref.shape[1]
    half = width // 2
    rows, cols = tile_hbm.shape[1:]
    pairs = (
        (measured_hbm, measured_ref),
        (tile_hbm, ext.at[:, half : half + rows, half : half + cols]),
        (top_hbm, ext.at[:, :half, half : half + cols]),
        (bottom_hbm, ext.at[:, half + rows :, half : half + cols]),
        (left_hbm, ext.at[:, :, :half]),
        (right_hbm, ext.at[:, :, half + cols :]),
    )
    loads = [pltpu.make_async_copy(src, dst, in_sems.at[i]) for i, (src, dst) in enumerate(pairs)]
    for load in loads:
        load.start()
    light_ref[...] = jnp.zeros_like(light_ref)

    @pl.loop(0, grad.shape[1] // 8)
    def _(step):
        at = pl.multiple_of(step * 8, 8)
        grad[:, pl.ds(at, 8), :] = jnp.zeros((2, 8, grad.shape[2]), F32)

    for load in loads:
        load.wait()

    def dot3(left, right):
        (lh, ll), (rh, rl) = left, right
        return dot(lh, rh) + dot(ll, rh) + dot(lh, rl)

    def table(which):
        return table_ref[which, 0], table_ref[which, 1]

    def put(which, at_rows, at_cols, value):
        high, low = halves(value)
        op_high[which, at_rows, at_cols] = high
        op_low[which, at_rows, at_cols] = low

    def operand(which):
        return op_high[which], op_low[which]

    whole = slice(None)
    near, far = slice(0, half), slice(half, width)

    def visit(slot, carry):
        row_at = offset_ref[slot, 0]
        col_at = offset_ref[slot, 1]
        row_base = pl.multiple_of((row_at // 8) * 8, 8)
        col_base = pl.multiple_of((col_at // 128) * 128, 128)
        row_by = row_at - row_base
        col_by = col_at - col_base
        lane = lax.broadcasted_iota(jnp.int32, (CHUNK, 128), 1) >= col_by
        sub = lax.broadcasted_iota(jnp.int32, (8, 128), 0) >= row_by

        def block(ref, part, first, count, piece):
            at = pl.multiple_of(col_base + piece * 128, 128)
            return ref[part, pl.ds(pl.multiple_of(row_base + first, 8), count), pl.ds(at, 128)]

        for part in (0, 1):
            turned = pltpu.roll(probe_ref[part], row_by, 0)
            probe_rot[part] = pltpu.roll(turned, col_by, 1)
        for first in range(0, width, CHUNK):
            here = slice(first, first + CHUNK)
            fields = []
            for part in (0, 1):
                pieces = []
                for piece in range(3):
                    body = block(ext, part, first, CHUNK, piece)
                    if first == 0:
                        tail = block(ext, part, width, 8, piece)
                        body = jnp.concatenate([jnp.where(sub, body[:8], tail), body[8:]], axis=0)
                    pieces.append(body)
                near_cols = jnp.where(lane, pieces[0], pieces[2])
                fields.append((near_cols, pieces[1]))
                win[part, here, near] = near_cols
                win[part, here, far] = pieces[1]
            exits = []
            for side, span in enumerate((near, far)):
                wr, wi = fields[0][side], fields[1][side]
                pr, pi = probe_rot[0, here, span], probe_rot[1, here, span]
                exits.append((pr * wr - pi * wi, pr * wi + pi * wr))
            for part, span in enumerate((near, far)):
                put(0, here, span, exits[0][part] + exits[1][part])
                put(1, here, span, exits[0][part] - exits[1][part])
        res[0] = dot3(operand(0), table(1))
        res[1] = dot3(operand(1), table(3))
        for part, rows_to in enumerate((near, far)):
            for parity, cols_to in enumerate((near, far)):
                upper = res[parity, near, rows_to]
                lower = res[parity, far, rows_to]
                put(0, rows_to, cols_to, upper + lower)
                put(1, rows_to, cols_to, upper - lower)
        res2[0] = dot3(table(0), operand(0))
        res2[1] = dot3(table(2), operand(1))
        for parity in (0, 1):
            re, im = res2[parity, near, :], res2[parity, far, :]
            rows_from = slice(parity * half, (parity + 1) * half)
            misfit = re * re + im * im - measured_ref[slot, rows_from, :]
            put(parity, near, whole, misfit * re)
            put(parity, far, whole, misfit * im)
        res[0] = dot3(table(1), operand(0))
        res[1] = dot3(table(3), operand(1))
        for part, cols_to in enumerate((near, far)):
            for parity, cols_from in enumerate((near, far)):
                first = res[0, cols_to, cols_from]
                second = res[1, cols_to, cols_from]
                put(parity, near, cols_to, first + second)
                put(parity, far, cols_to, first - second)
        res2[0] = dot3(operand(0), table(0))
        res2[1] = dot3(operand(1), table(2))
        for first in range(0, width, CHUNK):
            here = slice(first, first + CHUNK)
            terms = []
            for side, span in enumerate((near, far)):
                er, ei = res2[0, here, near], res2[0, here, far]
                dr, di = res2[1, here, near], res2[1, here, far]
                if side == 0:
                    br, bi = er + dr, ei + di
                else:
                    br, bi = er - dr, ei - di
                pr, pi = probe_rot[0, here, span], probe_rot[1, here, span]
                wr, wi = win[0, here, span], win[1, here, span]
                terms.append((pr * br + pi * bi, pr * bi - pi * br))
                win[0, here, span] = wr * br + wi * bi
                win[1, here, span] = wr * bi - wi * br

            def add(part, at, count, piece, value):
                to = pl.ds(pl.multiple_of(col_base + piece * 128, 128), 128)
                span = pl.ds(pl.multiple_of(row_base + at, 8), count)
                grad[part, span, to] = grad[part, span, to] + value

            for part in (0, 1):
                left_term = terms[0][part]
                right_term = terms[1][part]
                pieces = (
                    jnp.where(lane, left_term, 0.0),
                    right_term,
                    jnp.where(lane, 0.0, left_term),
                )
                for piece, value in enumerate(pieces):
                    if first == 0:
                        add(part, 0, 8, piece, jnp.where(sub, value[:8], 0.0))
                        add(part, 8, CHUNK - 8, piece, value[8:])
                        add(part, width, 8, piece, jnp.where(sub, 0.0, value[:8]))
                    else:
                        add(part, first, CHUNK, piece, value)
        for part in (0, 1):
            turned = pltpu.roll(win[part], lax.rem(width - col_by, width), 1)
            light_ref[part] = light_ref[part] + pltpu.roll(turned, lax.rem(width - row_by, width), 0)
        return carry

    lax.fori_loop(0, count_ref[0], visit, 0)
    out = pltpu.make_async_copy(grad, grad_hbm, out_sem)
    out.start()
    out.wait()


def patterns(counts, offsets, tables, probe, measured, tile, rims):
    width = probe.shape[1]
    rows, cols = tile.shape[1:]
    ext = (2, rows + width, cols + width)
    vmem = pl.BlockSpec(memory_space=pltpu.VMEM)
    smem = pl.BlockSpec(memory_space=pltpu.SMEM)
    hbm = pl.BlockSpec(memory_space=pl.ANY)
    return pl.pallas_call(
        patterns_kernel,
        in_specs=[smem, smem, vmem, vmem] + [hbm] * 6,
        out_specs=[hbm, vmem],
        out_shape=[jax.ShapeDtypeStruct(ext, F32), jax.ShapeDtypeStruct(probe.shape, F32)],
        scratch_shapes=[
            pltpu.VMEM(ext, F32),
            pltpu.VMEM(ext, F32),
            pltpu.VMEM(measured.shape, F32),
            pltpu.VMEM(probe.shape, F32),
            pltpu.VMEM(probe.shape, F32),
            pltpu.VMEM(probe.shape, BF16),
            pltpu.VMEM(probe.shape, BF16),
            pltpu.VMEM(probe.shape, F32),
            pltpu.VMEM(probe.shape, F32),
            pltpu.SemaphoreType.DMA((6,)),
            pltpu.SemaphoreType.DMA,
        ],
        compiler_params=pltpu.CompilerParams(vmem_limit_bytes=VMEM_LIMIT),
        name="patterns",
    )(counts, offsets, tables, probe, measured, tile, *rims)


def shifted(array, axis, by):
    size = lax.axis_size(axis)
    route = [(i, i + by) for i in range(size) if 0 <= i + by < size]
    return lax.ppermute(array, axis, route)


def fetch_rims(tile, half):
    rows, cols = tile.shape[1:]
    top = shifted(tile[:, rows - half :, :], "row", 1)
    bottom = shifted(tile[:, :half, :], "row", -1)
    edges = []
    for edge, by in ((slice(cols - half, cols), 1), (slice(0, half), -1)):
        strip = jnp.concatenate([top[:, :, edge], tile[:, :, edge], bottom[:, :, edge]], axis=1)
        edges.append(shifted(strip, "col", by))
    return top, bottom, edges[0], edges[1]


def fold_back(grad, half, rows, cols):
    from_right = shifted(grad[:, :, :half], "col", -1)
    from_left = shifted(grad[:, :, half + cols :], "col", 1)
    middle = grad[:, :, half : half + cols]
    middle = middle.at[:, :, :half].add(from_left)
    middle = middle.at[:, :, cols - half :].add(from_right)
    from_below = shifted(middle[:, :half, :], "row", -1)
    from_above = shifted(middle[:, half + rows :, :], "row", 1)
    inner = middle[:, half : half + rows, :]
    inner = inner.at[:, :half, :].add(from_above)
    return inner.at[:, rows - half :, :].add(from_below)


def per_device(object_field, illumination, measured, offsets, counts):
    width = illumination.shape[1]
    half = width // 2
    rows, cols = object_field.shape[1:]
    slots = measured.shape[0]
    total = slots * lax.axis_size("row") * lax.axis_size("col")
    tables = jnp.asarray(factor_tables(width))
    measured = reorder(measured, counts)
    tile, lighting = object_field, illumination
    for _ in range(ITERS):
        rims = fetch_rims(tile, half)
        grad, light = patterns(counts, offsets, tables, lighting, measured, tile, rims)
        tile = tile - OBJECT_RATE * fold_back(grad, half, rows, cols)
        lighting = lighting - (LIGHT_RATE / total) * lax.psum(light, ("row", "col"))
    return tile, lighting


def solution(mesh):
    placed = (
        P(None, "row", "col"),
        P(),
        P(("row", "col"), None, None),
        P(("row", "col"), None),
        P(("row", "col")),
    )
    return jax.shard_map(
        per_device,
        mesh=mesh,
        in_specs=placed,
        out_specs=(P(None, "row", "col"), P()),
        check_vma=False,
    )
```

```python
import functools
import math

import jax
import jax.numpy as jnp
import numpy as np
from jax import lax
from jax.experimental import pallas as pl
from jax.experimental.pallas import tpu as pltpu
from jax.sharding import PartitionSpec as P

ITERS = 2
OBJECT_RATE = 0.01
LIGHT_RATE = 0.02
MESH = pl.DeviceIdType.MESH
F32 = jnp.float32
BF16 = jnp.bfloat16
VMEM_LIMIT = 56 * 1024 * 1024


def halves(array):
    high = array.astype(BF16)
    low = (array - high.astype(F32)).astype(BF16)
    return high, low


def factor_tables(length):
    half = length // 2
    index = np.arange(half)
    found = []
    for parity in (0, 1):
        phase = ((2 * index[:, None] + parity) * index[None, :]) % length
        angle = phase * (2.0 * math.pi / length)
        real = np.cos(angle) / math.sqrt(length)
        imag = -np.sin(angle) / math.sqrt(length)
        whole = np.block([[real, -imag], [imag, real]])
        found += [whole, whole.T]
    split = []
    for matrix in found + [OBJECT_RATE * found[0], OBJECT_RATE * found[2]]:
        matrix = matrix.astype(np.float32)
        high = matrix.astype(jnp.bfloat16)
        low = (matrix - high.astype(np.float32)).astype(jnp.bfloat16)
        split.append(np.stack([high, low]))
    return np.stack(split)


def parity_order(length):
    half = length // 2
    order = np.zeros((length, length), np.float32)
    order[2 * np.arange(half), np.arange(half)] = 1
    order[2 * np.arange(half) + 1, half + np.arange(half)] = 1
    return order.astype(jnp.bfloat16)


def dot(left, right):
    return jnp.dot(left, right, preferred_element_type=F32)


CHUNK = 32


def margins(half, rows, cols):
    inner = slice(half, half + rows)
    return (
        (slice(0, half), slice(0, cols + 2 * half)),
        (slice(half + rows, rows + 2 * half), slice(0, cols + 2 * half)),
        (inner, slice(0, half)),
        (inner, slice(half + cols, cols + 2 * half)),
    )


def clear(ref, at_rows, at_cols):
    step = 8

    @pl.loop(at_rows.start, at_rows.stop, step=step)
    def _(i):
        at = pl.ds(pl.multiple_of(i, step), step)
        ref[:, at, at_cols] = jnp.zeros((2, step, at_cols.stop - at_cols.start), F32)


def patterns_kernel(rate, stepped, *refs):
    count_ref, offset_ref, edge_ref, table_ref, order_ref, probe_in = refs[:6]
    refs = refs[6:]
    if stepped:
        light_in, refs = refs[0], refs[1:]
    measured_hbm, tile_hbm, refs = refs[0], refs[1], refs[2:]
    if stepped:
        frame, refs = refs[:4], refs[4:]
    rims, refs = refs[:4], refs[4:]
    tile_out, *strips_out, light_out = refs[:6]
    (
        ext,
        new,
        measured_ref,
        target,
        probe_now,
        light_ref,
        probe_rot,
        win,
        op_high,
        op_low,
        res,
        res2,
        in_sems,
        out_sems,
    ) = refs[6:]
    width = probe_in.shape[1]
    half = width // 2
    rows, cols = tile_hbm.shape[1:]
    edges = margins(half, rows, cols)
    pairs = [(rim, ext.at[:, at[0], at[1]]) for rim, at in zip(rims, edges)]
    pairs += [
        (measured_hbm.at[:, :, side * half : (side + 1) * half], measured_ref.at[side])
        for side in (0, 1)
    ]
    for whole in (ext, new):
        core = whole.at[:, half : half + rows, half : half + cols]
        if stepped:
            core_rows, core_cols = slice(half, rows - half), slice(half, cols - half)
            pairs += [
                (frame[0], core.at[:, :, :half]),
                (frame[1], core.at[:, :, cols - half :]),
                (frame[2], core.at[:, :half, core_cols]),
                (frame[3], core.at[:, rows - half :, core_cols]),
                (tile_hbm.at[:, core_rows, core_cols], core.at[:, core_rows, core_cols]),
            ]
        else:
            pairs.append((tile_hbm, core))
    loads = [pltpu.make_async_copy(src, dst, in_sems.at[i]) for i, (src, dst) in enumerate(pairs)]
    for load in loads:
        load.start()
    light_ref[...] = jnp.zeros_like(light_ref)
    for at in edges:
        clear(new, *at)
    if stepped:
        step_probe(rate, probe_in, light_in, probe_now)
        probe_ref = probe_now
    else:
        probe_ref = probe_in
    for load in loads:
        load.wait()
    all_rows = slice(0, rows + width)
    beyond = (edges[0], edges[1], (all_rows, edges[2][1]), (all_rows, edges[3][1]))
    for i, at in enumerate(beyond):

        @pl.when(edge_ref[i] > 0)
        def _():
            clear(ext, *at)

    def dot3(left, right):
        (lh, ll), (rh, rl) = left, right
        return dot(lh, rh) + dot(ll, rh) + dot(lh, rl)

    def table(which):
        return table_ref[which, 0], table_ref[which, 1]

    def put(which, at_rows, at_cols, value):
        high, low = halves(value)
        op_high[which, at_rows, at_cols] = high
        op_low[which, at_rows, at_cols] = low

    def operand(which):
        return op_high[which], op_low[which]

    whole = slice(None)
    near, far = slice(0, half), slice(half, width)

    def visit(slot, carry):
        row_at = offset_ref[slot, 0]
        col_at = offset_ref[slot, 1]
        row_base = pl.multiple_of((row_at // 8) * 8, 8)
        col_base = pl.multiple_of((col_at // 128) * 128, 128)
        row_by = row_at - row_base
        col_by = col_at - col_base
        lane = lax.broadcasted_iota(jnp.int32, (CHUNK, 128), 1) >= col_by
        sub = lax.broadcasted_iota(jnp.int32, (8, 128), 0) >= row_by

        def block(ref, part, first, count, piece):
            at = pl.multiple_of(col_base + piece * 128, 128)
            return ref[part, pl.ds(pl.multiple_of(row_base + first, 8), count), pl.ds(at, 128)]

        for parity, to in enumerate((near, far)):
            picked = pl.ds(parity, half, stride=2)
            for side, span in enumerate((near, far)):
                put(0, to, span, measured_ref[side, slot, picked, :])
        target[...] = dot(op_high[0], order_ref[...]) + dot(op_low[0], order_ref[...])
        for part in (0, 1):
            turned = pltpu.roll(probe_ref[part], row_by, 0)
            probe_rot[part] = pltpu.roll(turned, col_by, 1)
        for first in range(0, width, CHUNK):
            here = slice(first, first + CHUNK)
            fields = []
            for part in (0, 1):
                pieces = []
                for piece in range(3):
                    body = block(ext, part, first, CHUNK, piece)
                    if first == 0:
                        tail = block(ext, part, width, 8, piece)
                        body = jnp.concatenate([jnp.where(sub, body[:8], tail), body[8:]], axis=0)
                    pieces.append(body)
                near_cols = jnp.where(lane, pieces[0], pieces[2])
                fields.append((near_cols, pieces[1]))
                win[part, here, near] = near_cols
                win[part, here, far] = pieces[1]
            exits = []
            for side, span in enumerate((near, far)):
                wr, wi = fields[0][side], fields[1][side]
                pr, pi = probe_rot[0, here, span], probe_rot[1, here, span]
                exits.append((pr * wr - pi * wi, pr * wi + pi * wr))
            for part, span in enumerate((near, far)):
                put(0, here, span, exits[0][part] + exits[1][part])
                put(1, here, span, exits[0][part] - exits[1][part])
        res[0] = dot3(operand(0), table(1))
        res[1] = dot3(operand(1), table(3))
        for part, rows_to in enumerate((near, far)):
            for parity, cols_to in enumerate((near, far)):
                upper = res[parity, near, rows_to]
                lower = res[parity, far, rows_to]
                put(0, rows_to, cols_to, upper + lower)
                put(1, rows_to, cols_to, upper - lower)
        res2[0] = dot3(table(0), operand(0))
        res2[1] = dot3(table(2), operand(1))
        for parity in (0, 1):
            re, im = res2[parity, near, :], res2[parity, far, :]
            rows_from = slice(parity * half, (parity + 1) * half)
            misfit = re * re + im * im - target[rows_from, :]
            put(parity, near, whole, misfit * re)
            put(parity, far, whole, misfit * im)
        res[0] = dot3(table(1), operand(0))
        res[1] = dot3(table(3), operand(1))
        for part, cols_to in enumerate((near, far)):
            for parity, cols_from in enumerate((near, far)):
                first = res[0, cols_to, cols_from]
                second = res[1, cols_to, cols_from]
                put(parity, near, cols_to, first + second)
                put(parity, far, cols_to, first - second)
        res2[0] = dot3(operand(0), table(4))
        res2[1] = dot3(operand(1), table(5))
        for first in range(0, width, CHUNK):
            here = slice(first, first + CHUNK)
            terms = []
            for side, span in enumerate((near, far)):
                er, ei = res2[0, here, near], res2[0, here, far]
                dr, di = res2[1, here, near], res2[1, here, far]
                if side == 0:
                    br, bi = er + dr, ei + di
                else:
                    br, bi = er - dr, ei - di
                pr, pi = probe_rot[0, here, span], probe_rot[1, here, span]
                wr, wi = win[0, here, span], win[1, here, span]
                terms.append((pr * br + pi * bi, pr * bi - pi * br))
                win[0, here, span] = wr * br + wi * bi
                win[1, here, span] = wr * bi - wi * br

            def take(part, at, count, piece, value):
                to = pl.ds(pl.multiple_of(col_base + piece * 128, 128), 128)
                span = pl.ds(pl.multiple_of(row_base + at, 8), count)
                new[part, span, to] = new[part, span, to] - value

            for part in (0, 1):
                left_term = terms[0][part]
                right_term = terms[1][part]
                pieces = (
                    jnp.where(lane, left_term, 0.0),
                    right_term,
                    jnp.where(lane, 0.0, left_term),
                )
                for piece, value in enumerate(pieces):
                    if first == 0:
                        take(part, 0, 8, piece, jnp.where(sub, value[:8], 0.0))
                        take(part, 8, CHUNK - 8, piece, value[8:])
                        take(part, width, 8, piece, jnp.where(sub, 0.0, value[:8]))
                    else:
                        take(part, first, CHUNK, piece, value)
        for part in (0, 1):
            turned = pltpu.roll(win[part], lax.rem(width - col_by, width), 1)
            light_ref[part] = light_ref[part] + pltpu.roll(turned, lax.rem(width - row_by, width), 0)
        return carry

    lax.fori_loop(0, count_ref[0], visit, 0)
    pairs = [(new.at[:, half : half + rows, half : half + cols], tile_out)]
    pairs += [(new.at[:, at[0], at[1]], out) for at, out in zip(edges, strips_out)]
    stores = [pltpu.make_async_copy(src, dst, out_sems.at[i]) for i, (src, dst) in enumerate(pairs)]
    for store in stores:
        store.start()
    per_part = width // 8
    for part in (0, 1):

        @pl.loop(0, per_part)
        def _(i):
            span = pl.ds(pl.multiple_of(i * 8, 8), 8)
            for side in (0, 1):
                lanes = slice(side * 128, (side + 1) * 128)
                light_out[(part * per_part + i) * 2 + side] = light_ref[part, span, lanes]

    for store in stores:
        store.wait()


def patterns(
    counts, offsets, edges, tables, order, probe, sums, measured, tile, frame, rims, rate
):
    width = probe.shape[1]
    half = width // 2
    rows, cols = tile.shape[1:]
    ext = (2, rows + width, cols + width)
    flat, tall = (2, half, cols + width), (2, rows, half)
    vmem = pl.BlockSpec(memory_space=pltpu.VMEM)
    smem = pl.BlockSpec(memory_space=pltpu.SMEM)
    hbm = pl.BlockSpec(memory_space=pl.ANY)
    stepped = len(sums) > 0
    units = 2 * width * width // 1024
    outs = [tile.shape, flat, flat, tall, tall, (units, 8, 128)]
    return pl.pallas_call(
        functools.partial(patterns_kernel, rate, stepped),
        in_specs=[smem] * 3 + [vmem] * (3 + len(sums)) + [hbm] * (6 + len(frame)),
        out_specs=[hbm] * 5 + [vmem],
        out_shape=[jax.ShapeDtypeStruct(shape, F32) for shape in outs],
        scratch_shapes=[
            pltpu.VMEM(ext, F32),
            pltpu.VMEM(ext, F32),
            pltpu.VMEM((2, measured.shape[0], width, half), F32),
            pltpu.VMEM((width, width), F32),
            pltpu.VMEM(probe.shape, F32),
            pltpu.VMEM(probe.shape, F32),
            pltpu.VMEM(probe.shape, F32),
            pltpu.VMEM(probe.shape, F32),
            pltpu.VMEM(probe.shape, BF16),
            pltpu.VMEM(probe.shape, BF16),
            pltpu.VMEM(probe.shape, F32),
            pltpu.VMEM(probe.shape, F32),
            pltpu.SemaphoreType.DMA((16,)),
            pltpu.SemaphoreType.DMA((5,)),
        ],
        compiler_params=pltpu.CompilerParams(vmem_limit_bytes=VMEM_LIMIT),
        name="patterns",
    )(counts, offsets, edges, tables, order, probe, *sums, measured, tile, *frame, *rims)


class Exchange:
    def __init__(self, send_sems, recv_sems):
        self.sems = (send_sems, recv_sems)
        self.used = 0
        self.open = []

    def send(self, src, dst, to, landing=None):
        at = self.used
        self.used += 1
        copy = self.describe(src, dst, to, at)
        copy.start()
        arrival = copy if landing is None else self.describe(src, landing, to, at)
        self.open.append(copy)
        return arrival.wait_recv

    def describe(self, src, dst, to, at):
        return pltpu.make_async_remote_copy(
            src_ref=src,
            dst_ref=dst,
            send_sem=self.sems[0].at[at],
            recv_sem=self.sems[1].at[at],
            device_id=to,
            device_id_type=MESH,
        )

    def finish(self):
        for copy in self.open:
            copy.wait_send()


def greet(peers):
    barrier = pltpu.get_barrier_semaphore()
    for peer in peers:
        pl.semaphore_signal(barrier, inc=1, device_id=peer, device_id_type=MESH)
    pl.semaphore_wait(barrier, len(peers))


class Place:
    def __init__(self, mesh_shape):
        self.n_row, self.n_col = mesh_shape
        self.row = lax.axis_index("row")
        self.col = lax.axis_index("col")
        self.up = (lax.rem(self.row + self.n_row - 1, self.n_row), self.col)
        self.down = (lax.rem(self.row + 1, self.n_row), self.col)
        self.left = (self.row, lax.rem(self.col + self.n_col - 1, self.n_col))
        self.right = (self.row, lax.rem(self.col + 1, self.n_col))

    def near(self):
        return [self.up, self.down, self.left, self.right]

    def reducers(self):
        core = lax.rem(self.row, 2)
        partner = (self.row + 1 - 2 * core, self.col)
        along = [
            (lax.rem(self.row + 2 * j, self.n_row), self.col) for j in range(1, self.n_row // 2)
        ]
        across = [(self.row, lax.rem(self.col + j, self.n_col)) for j in range(1, self.n_col)]
        return partner, along, across


def probe_sum(place, net, light, total, first, second, got_core, got_row, got_col):
    partner, along, across = place.reducers()
    core, x = lax.rem(place.row, 2), lax.div(place.row, 2)
    n_x, n_col = place.n_row // 2, place.n_col
    big, mid = first.shape[0], second.shape[0]
    arrive = net.send(light.at[pl.ds((1 - core) * big, big)], got_core, partner)
    yield
    arrive()

    @pl.loop(0, big)
    def _(i):
        first[i] = light[core * big + i] + got_core[i]

    waits = []
    for j, peer in enumerate(along):
        there = lax.div(peer[0], 2)
        waits.append(net.send(first.at[pl.ds(there * mid, mid)], got_row.at[j], peer))
    yield
    for wait in waits:
        wait()

    @pl.loop(0, mid)
    def _(i):
        value = first[x * mid + i]
        for j in range(n_x - 1):
            value = value + got_row[j, i]
        second[i] = value

    waits = [net.send(second.at[peer[1]], got_col.at[j], peer) for j, peer in enumerate(across)]
    yield
    for wait in waits:
        wait()
    value = second[place.col]
    for j in range(n_col - 1):
        value = value + got_col[j]
    corner = core * big + x * mid
    mine = corner + place.col
    total[mine] = value
    waits = []
    for j, peer in enumerate(across):
        source = lax.rem(place.col + n_col - (j + 1), n_col)
        waits.append(net.send(total.at[mine], total.at[mine], peer, total.at[corner + source]))
    yield
    for wait in waits:
        wait()
    block = pl.ds(corner, mid)
    waits = []
    for j, peer in enumerate(along):
        source = lax.rem(x + n_x - (j + 1), n_x)
        landing = total.at[pl.ds(core * big + source * mid, mid)]
        waits.append(net.send(total.at[block], total.at[block], peer, landing))
    yield
    for wait in waits:
        wait()
    block = pl.ds(core * big, big)
    landing = total.at[pl.ds((1 - core) * big, big)]
    arrive = net.send(total.at[block], total.at[block], partner, landing)
    yield
    arrive()


def fetch_kernel(mesh_shape, half, tile, top, bottom, left, right, send_sems, recv_sems):
    place = Place(mesh_shape)
    net = Exchange(send_sems, recv_sems)
    rows, cols = tile.shape[1:]
    greet(place.near())
    ends = (slice(0, half), slice(rows - half, rows))
    first, last = slice(0, half), slice(cols - half, cols)
    inner = slice(half, half + cols)
    waits = []
    for end in ends:
        waits.append(net.send(tile.at[:, end, first], right.at[:, end], place.left))
        waits.append(net.send(tile.at[:, end, last], left.at[:, end], place.right))
    later = [
        net.send(tile.at[:, ends[0]], bottom.at[:, :, inner], place.up),
        net.send(tile.at[:, ends[1]], top.at[:, :, inner], place.down),
    ]
    middle = slice(half, rows - half)
    later.append(net.send(tile.at[:, middle, first], right.at[:, middle], place.left))
    later.append(net.send(tile.at[:, middle, last], left.at[:, middle], place.right))
    for wait in waits:
        wait()
    outer = (slice(0, half), slice(half + cols, 2 * half + cols))
    for rim, to in zip((left, right), outer):
        later.append(net.send(rim.at[:, ends[0]], bottom.at[:, :, to], place.up))
        later.append(net.send(rim.at[:, ends[1]], top.at[:, :, to], place.down))
    for wait in later:
        wait()
    net.finish()


def fetch_rims(mesh_shape, tile, half):
    rows, cols = tile.shape[1:]
    flat = jax.ShapeDtypeStruct((2, half, cols + 2 * half), F32)
    tall = jax.ShapeDtypeStruct((2, rows, half), F32)
    hbm = pl.BlockSpec(memory_space=pl.ANY)
    return pl.pallas_call(
        functools.partial(fetch_kernel, mesh_shape, half),
        in_specs=[hbm],
        out_specs=[hbm] * 4,
        out_shape=[flat, flat, tall, tall],
        scratch_shapes=[pltpu.SemaphoreType.DMA((12,)), pltpu.SemaphoreType.DMA((12,))],
        compiler_params=pltpu.CompilerParams(collective_id=1, has_side_effects=True),
        name="fetch_rims",
    )(tile)


def add_rows(target, at_rows, source, from_rows, from_cols):
    step = 32

    @pl.loop(0, at_rows.stop - at_rows.start, step=step)
    def _(i):
        to = pl.ds(pl.multiple_of(at_rows.start + i, step), step)
        here = pl.ds(pl.multiple_of(from_rows.start + i, step), step)
        target[:, to, :] = target[:, to, :] + source[:, here, from_cols]


def settle_kernel(mesh_shape, half, again, *refs):
    tile, grad_top, grad_bottom, grad_left, grad_right, light = refs[:6]
    refs = refs[6:]
    out_left, out_right, out_top, out_bottom, total_out = refs[:5]
    refs = refs[5:]
    if again:
        top, bottom, left, right = refs[:4]
        refs = refs[4:]
    (
        own_left,
        own_right,
        own_top,
        own_bottom,
        end_left,
        end_right,
        got_top,
        got_bottom,
        got_left,
        got_right,
        total,
        first_sum,
        second_sum,
        got_core,
        got_row,
        got_col,
        load_sems,
        send_sems,
        recv_sems,
    ) = refs
    place = Place(mesh_shape)
    net = Exchange(send_sems, recv_sems)
    rows, cols = tile.shape[1:]
    partner, along, across = place.reducers()
    further = (lax.rem(place.row + place.n_row - 1 + 2 * lax.rem(place.row, 2), place.n_row), place.col)
    greet([partner, further] + along + across)

    up_end, down_end = slice(0, half), slice(rows - half, rows)
    split = (rows - 2 * half) // 2 + half
    middles = (slice(half, split), slice(split, rows - half))
    first, last = slice(0, half), slice(cols - half, cols)
    core_cols = slice(half, cols - half)
    row_waits = [
        net.send(grad_top, got_bottom, place.up),
        net.send(grad_bottom, got_top, place.down),
    ]
    part = middles[0]
    mid_waits = [
        [
            net.send(grad_left.at[:, part], got_right.at[:, part], place.left),
            net.send(grad_right.at[:, part], got_left.at[:, part], place.right),
        ]
    ]
    pairs = (
        (grad_left.at[:, up_end], end_left.at[0]),
        (grad_left.at[:, down_end], end_left.at[1]),
        (grad_right.at[:, up_end], end_right.at[0]),
        (grad_right.at[:, down_end], end_right.at[1]),
        (tile.at[:, :, first], own_left),
        (tile.at[:, :, last], own_right),
        (tile.at[:, up_end, core_cols], own_top),
        (tile.at[:, down_end, core_cols], own_bottom),
    )
    loads = [pltpu.make_async_copy(src, dst, load_sems.at[i]) for i, (src, dst) in enumerate(pairs)]
    for load in loads:
        load.start()
    sums = probe_sum(place, net, light, total, first_sum, second_sum, got_core, got_row, got_col)
    next(sums)
    for load in loads:
        load.wait()
    next(sums)
    for wait in row_waits:
        wait()
    whole = slice(0, half)
    wide = (slice(0, half), slice(half, 2 * half), slice(2 * half, cols), slice(cols, cols + half))
    wide = wide + (slice(cols + half, cols + 2 * half),)
    for end, (got, own, span, inside) in enumerate(
        (
            (got_top, own_top, up_end, place.row > 0),
            (got_bottom, own_bottom, down_end, place.row < place.n_row - 1),
        )
    ):

        @pl.when(inside)
        def _():
            add_rows(end_left.at[end], whole, got, whole, wide[0])
            add_rows(own_left, span, got, whole, wide[1])
            add_rows(own, whole, got, whole, wide[2])
            add_rows(own_right, span, got, whole, wide[3])
            add_rows(end_right.at[end], whole, got, whole, wide[4])

    end_waits = []
    for end, span in enumerate((up_end, down_end)):
        end_waits.append(net.send(end_left.at[end], got_right.at[:, span], place.left))
        end_waits.append(net.send(end_right.at[end], got_left.at[:, span], place.right))
    part = middles[1]
    mid_waits.append(
        [
            net.send(grad_left.at[:, part], got_right.at[:, part], place.left),
            net.send(grad_right.at[:, part], got_left.at[:, part], place.right),
        ]
    )
    next(sums)
    next(sums)

    def take_cols(span):
        @pl.when(place.col > 0)
        def _():
            add_rows(own_left, span, got_left, span, slice(None))

        @pl.when(place.col < place.n_col - 1)
        def _():
            add_rows(own_right, span, got_right, span, slice(None))

    def give_cols(span):
        return [
            net.send(own_left.at[:, span], right.at[:, span], place.left),
            net.send(own_right.at[:, span], left.at[:, span], place.right),
        ]

    later, corner_waits = [], []
    for wait in mid_waits[0]:
        wait()
    take_cols(middles[0])
    next(sums)
    for wait in end_waits:
        wait()
    take_cols(up_end)
    take_cols(down_end)
    if again:
        corner_waits = give_cols(up_end) + give_cols(down_end)
        for span, own, rim, to in (
            (up_end, own_top, bottom, place.up),
            (down_end, own_bottom, top, place.down),
        ):
            later.append(net.send(own_left.at[:, span], rim.at[:, :, wide[1]], to))
            later.append(net.send(own, rim.at[:, :, wide[2]], to))
            later.append(net.send(own_right.at[:, span], rim.at[:, :, wide[3]], to))
        later += give_cols(middles[0])
    next(sums)
    for wait in mid_waits[1]:
        wait()
    take_cols(middles[1])
    if again:
        later += give_cols(middles[1])
    for _ in sums:
        pass
    if again:
        for wait in corner_waits:
            wait()
        for rim, to in ((left, wide[0]), (right, wide[4])):
            later.append(net.send(rim.at[:, up_end], bottom.at[:, :, to], place.up))
            later.append(net.send(rim.at[:, down_end], top.at[:, :, to], place.down))
    stores = [
        pltpu.make_async_copy(src, dst, load_sems.at[i])
        for i, (src, dst) in enumerate(
            (
                (own_left, out_left),
                (own_right, out_right),
                (own_top, out_top),
                (own_bottom, out_bottom),
                (total, total_out),
            )
        )
    ]
    for store in stores:
        store.start()
    for wait in later:
        wait()
    net.finish()
    for store in stores:
        store.wait()


def settle(mesh_shape, tile, strips, light, again):
    rows, cols = tile.shape[1:]
    half = strips[2].shape[2]
    n_row, n_col = mesh_shape
    big, mid = light.shape[0] // 2, light.shape[0] // n_row
    unit = light.shape[1:]
    flat, tall = (2, half, cols + 2 * half), (2, rows, half)
    inner, ends = (2, half, cols - 2 * half), (2, 2, half, half)
    outs = [tall, tall, inner, inner, light.shape] + ([flat, flat, tall, tall] if again else [])
    copies = 2 + 4 + 4 + 2 + 2 * (n_col - 1) + 2 * (n_row // 2 - 1) + (18 if again else 0)
    hbm = pl.BlockSpec(memory_space=pl.ANY)
    vmem = pl.BlockSpec(memory_space=pltpu.VMEM)
    return pl.pallas_call(
        functools.partial(settle_kernel, mesh_shape, half, again),
        in_specs=[hbm] * 5 + [vmem],
        out_specs=[hbm] * len(outs),
        out_shape=[jax.ShapeDtypeStruct(shape, F32) for shape in outs],
        scratch_shapes=[
            pltpu.VMEM(tall, F32),
            pltpu.VMEM(tall, F32),
            pltpu.VMEM(inner, F32),
            pltpu.VMEM(inner, F32),
            pltpu.VMEM(ends, F32),
            pltpu.VMEM(ends, F32),
            pltpu.VMEM(flat, F32),
            pltpu.VMEM(flat, F32),
            pltpu.VMEM(tall, F32),
            pltpu.VMEM(tall, F32),
            pltpu.VMEM(light.shape, F32),
            pltpu.VMEM((big,) + unit, F32),
            pltpu.VMEM((mid,) + unit, F32),
            pltpu.VMEM((big,) + unit, F32),
            pltpu.VMEM((n_row // 2 - 1, mid) + unit, F32),
            pltpu.VMEM((n_col - 1,) + unit, F32),
            pltpu.SemaphoreType.DMA((8,)),
            pltpu.SemaphoreType.DMA((copies,)),
            pltpu.SemaphoreType.DMA((copies,)),
        ],
        compiler_params=pltpu.CompilerParams(
            collective_id=2 if again else 3, has_side_effects=True, vmem_limit_bytes=VMEM_LIMIT
        ),
        name="settle_and_fetch" if again else "settle",
    )(tile, *strips, light)


def finish_kernel(rate, *refs):
    probe, sum_first, sum_last, left, right, top, bottom, tile_in, tile, probe_out, sems = refs
    rows, cols = tile.shape[1:]
    half = left.shape[2]
    first, last, core_cols = slice(0, half), slice(cols - half, cols), slice(half, cols - half)
    pairs = (
        (left, tile.at[:, :, first]),
        (right, tile.at[:, :, last]),
        (top, tile.at[:, :half, core_cols]),
        (bottom, tile.at[:, rows - half :, core_cols]),
    )
    stores = [pltpu.make_async_copy(src, dst, sems.at[i]) for i, (src, dst) in enumerate(pairs)]
    for store in stores:
        store.start()
    step_probe(rate, probe, sum_first, probe_out)
    step_probe(rate, probe_out, sum_last, probe_out)
    for store in stores:
        store.wait()


def finish(probe, sums, frame, tile, rate):
    hbm = pl.BlockSpec(memory_space=pl.ANY)
    vmem = pl.BlockSpec(memory_space=pltpu.VMEM)
    return pl.pallas_call(
        functools.partial(finish_kernel, rate),
        in_specs=[vmem] * 3 + [hbm] * 5,
        out_specs=[hbm, vmem],
        out_shape=[
            jax.ShapeDtypeStruct(tile.shape, F32),
            jax.ShapeDtypeStruct(probe.shape, F32),
        ],
        scratch_shapes=[pltpu.SemaphoreType.DMA((4,))],
        input_output_aliases={7: 0},
        compiler_params=pltpu.CompilerParams(vmem_limit_bytes=VMEM_LIMIT),
        name="finish",
    )(probe, *sums, *frame, tile)


def step_probe(rate, probe, light, out):
    width = probe.shape[1]
    per_part = width // 8
    for part in (0, 1):

        @pl.loop(0, per_part)
        def _(i):
            span = pl.ds(pl.multiple_of(i * 8, 8), 8)
            for side in (0, 1):
                lanes = slice(side * 128, (side + 1) * 128)
                block = light[(part * per_part + i) * 2 + side]
                out[part, span, lanes] = probe[part, span, lanes] - rate * block


def per_device(mesh_shape, object_field, illumination, measured, offsets, counts):
    width = illumination.shape[1]
    half = width // 2
    total = measured.shape[0] * mesh_shape[0] * mesh_shape[1]
    rate = LIGHT_RATE / total / OBJECT_RATE
    tables = jnp.asarray(factor_tables(width))
    order = jnp.asarray(parity_order(width))
    row, col = lax.axis_index("row"), lax.axis_index("col")
    edges = jnp.stack(
        [row == 0, row == mesh_shape[0] - 1, col == 0, col == mesh_shape[1] - 1]
    ).astype(jnp.int32)
    sums = []
    tile, frame, probe = object_field, (), illumination
    rims = fetch_rims(mesh_shape, tile, half)
    for sweep in range(ITERS):
        tile, *strips, light = patterns(
            counts, offsets, edges, tables, order, probe, sums, measured, tile, frame, rims, rate
        )
        found = settle(mesh_shape, tile, strips, light, sweep < ITERS - 1)
        frame, rims = found[:4], found[5:]
        sums.append(found[4])
    return finish(probe, sums, frame, tile, rate)


def solution(mesh):
    placed = (
        P(None, "row", "col"),
        P(),
        P(("row", "col"), None, None),
        P(("row", "col"), None),
        P(("row", "col")),
    )
    mesh_shape = (mesh.shape["row"], mesh.shape["col"])
    return jax.shard_map(
        functools.partial(per_device, mesh_shape),
        mesh=mesh,
        in_specs=placed,
        out_specs=(P(None, "row", "col"), P()),
        check_vma=False,
    )
```

```python
import functools
import math

import jax
import jax.numpy as jnp
import numpy as np
from jax import lax
from jax.experimental import pallas as pl
from jax.experimental.pallas import tpu as pltpu
from jax.sharding import PartitionSpec as P

ITERS = 2
OBJECT_RATE = 0.01
LIGHT_RATE = 0.02
MESH = pl.DeviceIdType.MESH
F32 = jnp.float32
BF16 = jnp.bfloat16
MIB = 1024 * 1024


def halves(array):
    high = array.astype(BF16)
    low = (array - high.astype(F32)).astype(BF16)
    return high, low


def factor_tables(length):
    half = length // 2
    index = np.arange(half)
    found = []
    for parity in (0, 1):
        phase = ((2 * index[:, None] + parity) * index[None, :]) % length
        angle = phase * (2.0 * math.pi / length)
        real = np.cos(angle) / math.sqrt(length)
        imag = -np.sin(angle) / math.sqrt(length)
        whole = np.block([[real, -imag], [imag, real]])
        found += [whole, whole.T]
    split = []
    for matrix in found + [OBJECT_RATE * found[0], OBJECT_RATE * found[2]]:
        matrix = matrix.astype(np.float32)
        high = matrix.astype(jnp.bfloat16)
        low = (matrix - high.astype(np.float32)).astype(jnp.bfloat16)
        split.append(np.stack([high, low]))
    return np.stack(split)


def parity_order(length):
    half = length // 2
    order = np.zeros((length, length), np.float32)
    order[2 * np.arange(half), np.arange(half)] = 1
    order[2 * np.arange(half) + 1, half + np.arange(half)] = 1
    return order.astype(jnp.bfloat16)


def dot(left, right):
    return jnp.dot(left, right, preferred_element_type=F32)


CHUNK = 32
STAGGER = 1
TOGETHER = 3


def margins(half, rows, cols):
    inner = slice(half, half + rows)
    return (
        (slice(0, half), slice(0, cols + 2 * half)),
        (slice(half + rows, rows + 2 * half), slice(0, cols + 2 * half)),
        (inner, slice(0, half)),
        (inner, slice(half + cols, cols + 2 * half)),
    )


def frame_parts(half, rows, cols):
    inner = slice(half, cols - half)
    return (
        (slice(0, rows), slice(0, half)),
        (slice(0, rows), slice(cols - half, cols)),
        (slice(0, half), inner),
        (slice(rows - half, rows), inner),
    )


def clear(ref, at_rows, at_cols):
    step = 8

    @pl.loop(at_rows.start, at_rows.stop, step=step)
    def _(i):
        at = pl.ds(pl.multiple_of(i, step), step)
        ref[:, at, at_cols] = jnp.zeros((2, step, at_cols.stop - at_cols.start), F32)


def patterns_kernel(mesh_shape, rate, stepped, *refs):
    count_ref, offset_ref, table_ref, order_ref, probe_in = refs[:5]
    refs = refs[5:]
    if stepped:
        light_in, refs = refs[0], refs[1:]
    measured_hbm, tile_hbm, refs = refs[0], refs[1], refs[2:]
    if stepped:
        frame, refs = refs[:4], refs[4:]
    rims, refs = refs[:4], refs[4:]
    tile_out, *sides_out, light_out = refs[:10]
    (
        ext,
        new,
        measured_ref,
        probe_now,
        light_ref,
        *banks,
        in_sems,
        out_sems,
    ) = refs[10:]
    width = probe_in.shape[1]
    half = width // 2
    rows, cols = tile_hbm.shape[1:]
    edges = margins(half, rows, cols)
    borders = frame_parts(half, rows, cols)
    pairs = [(rim, ext.at[:, at[0], at[1]]) for rim, at in zip(rims, edges)]
    pairs += [
        (measured_hbm.at[:, :, side * half : (side + 1) * half], measured_ref.at[side])
        for side in (0, 1)
    ]
    for whole in (ext, new):
        core = whole.at[:, half : half + rows, half : half + cols]
        if stepped:
            core_rows, core_cols = slice(half, rows - half), slice(half, cols - half)
            pairs += [(part, core.at[:, at[0], at[1]]) for part, at in zip(frame, borders)]
            pairs.append((tile_hbm.at[:, core_rows, core_cols], core.at[:, core_rows, core_cols]))
        else:
            pairs.append((tile_hbm, core))
    loads = [pltpu.make_async_copy(src, dst, in_sems.at[i]) for i, (src, dst) in enumerate(pairs)]
    for load in loads:
        load.start()
    light_ref[...] = jnp.zeros_like(light_ref)
    for at in edges:
        clear(new, *at)
    probe_ref = probe_now
    if stepped:
        step_probe(rate, probe_in, light_in, probe_now, 8)
    else:
        probe_now[:, 8:, :] = probe_in[...]
    probe_now[:, :8, :] = probe_now[:, width:, :]
    split = 6 + (len(loads) - 6) // 2
    waiting = loads[split:]
    for load in loads[:split]:
        load.wait()
    all_rows = slice(0, rows + width)
    beyond = (edges[0], edges[1], (all_rows, edges[2][1]), (all_rows, edges[3][1]))
    row, col = lax.axis_index("row"), lax.axis_index("col")
    outside = (row == 0, row == mesh_shape[0] - 1, col == 0, col == mesh_shape[1] - 1)
    for i, at in enumerate(beyond):

        @pl.when(outside[i])
        def _():
            clear(ext, *at)

    def dot3(left, right):
        (lh, ll), (rh, rl) = left, right
        return dot(jnp.concatenate([lh, ll, lh], axis=1), jnp.concatenate([rh, rh, rl], axis=0))

    def table(which):
        return table_ref[which, 0], table_ref[which, 1]

    whole = slice(None)
    near, far = slice(0, half), slice(half, width)

    def visit(slot, live, bank, arrived):
        op_high, op_low, res, win, probe_rot, target, order_high, order_low = (ref.at[bank] for ref in banks)

        def put(which, at_rows, at_cols, value):
            high, low = halves(value)
            op_high[which, at_rows, at_cols] = high
            op_low[which, at_rows, at_cols] = low

        def operand(which):
            return op_high[which], op_low[which]

        row_at = offset_ref[0, slot]
        col_at = offset_ref[1, slot]
        row_base = pl.multiple_of((row_at // 8) * 8, 8)
        col_base = pl.multiple_of((col_at // 128) * 128, 128)
        row_by = row_at - row_base
        col_by = col_at - col_base
        first_lanes = lax.broadcasted_iota(jnp.int32, (CHUNK, half), 1)
        first_rows = lax.broadcasted_iota(jnp.int32, (8, half), 0)
        lane = first_lanes >= col_by
        sub = first_rows >= row_by

        def block(ref, part, first, count, piece):
            at = pl.multiple_of(col_base + piece * 128, 128)
            return ref[part, pl.ds(pl.multiple_of(row_base + first, 8), count), pl.ds(at, 128)]

        for parity, to in enumerate((near, far)):
            picked = pl.ds(parity, half, stride=2)
            for side, span in enumerate((near, far)):
                high, low = halves(measured_ref[side, slot, picked, :])
                order_high[to, span] = high
                order_low[to, span] = low
        yield
        target[...] = dot(order_high[...], order_ref[...]) + dot(order_low[...], order_ref[...])
        above = (first_rows >= row_by)[None]
        lane_in = first_lanes >= col_by
        for part in (0, 1):
            for first in range(0, width, CHUNK):
                sides = []
                for span in (near, far):
                    block8 = probe_ref[part, first : first + CHUNK + 8, span]
                    block8 = pltpu.roll(block8.reshape(-1, 8, half), row_by, 1)
                    block8 = jnp.where(above, block8[1:], block8[:-1]).reshape(CHUNK, half)
                    sides.append(pltpu.roll(block8, col_by, 1))
                here = slice(first, first + CHUNK)
                probe_rot[part, here, near] = jnp.where(lane_in, sides[0], sides[1])
                probe_rot[part, here, far] = jnp.where(lane_in, sides[1], sides[0])
        yield
        for first in range(0, width, CHUNK):
            here = slice(first, first + CHUNK)
            fields = []
            for part in (0, 1):
                pieces = []
                for piece in range(3):
                    body = block(ext, part, first, CHUNK, piece)
                    if first == 0:
                        tail = block(ext, part, width, 8, piece)
                        body = jnp.concatenate([jnp.where(sub, body[:8], tail), body[8:]], axis=0)
                    pieces.append(body)
                near_cols = jnp.where(lane, pieces[0], pieces[2])
                fields.append((near_cols, pieces[1]))
                win[part, here, near] = near_cols
                win[part, here, far] = pieces[1]
            exits = []
            for side, span in enumerate((near, far)):
                wr, wi = fields[0][side], fields[1][side]
                pr, pi = probe_rot[0, here, span], probe_rot[1, here, span]
                exits.append((pr * wr - pi * wi, pr * wi + pi * wr))
            for part, span in enumerate((near, far)):
                put(0, here, span, exits[0][part] + exits[1][part])
                put(1, here, span, exits[0][part] - exits[1][part])
        yield
        res[0] = dot3(operand(0), table(1))
        res[1] = dot3(operand(1), table(3))
        yield
        for part, rows_to in enumerate((near, far)):
            for parity, cols_to in enumerate((near, far)):
                upper = res[parity, near, rows_to]
                lower = res[parity, far, rows_to]
                put(0, rows_to, cols_to, upper + lower)
                put(1, rows_to, cols_to, upper - lower)
        yield
        res[0] = dot3(table(0), operand(0))
        res[1] = dot3(table(2), operand(1))
        yield
        for parity in (0, 1):
            re, im = res[parity, near, :], res[parity, far, :]
            rows_from = slice(parity * half, (parity + 1) * half)
            misfit = re * re + im * im - target[rows_from, :]
            misfit = jnp.where(live, misfit, 0.0)
            put(parity, near, whole, misfit * re)
            put(parity, far, whole, misfit * im)
        yield
        res[0] = dot3(table(1), operand(0))
        res[1] = dot3(table(3), operand(1))
        yield
        for part, cols_to in enumerate((near, far)):
            for parity, cols_from in enumerate((near, far)):
                first = res[0, cols_to, cols_from]
                second = res[1, cols_to, cols_from]
                put(parity, near, cols_to, first + second)
                put(parity, far, cols_to, first - second)
        yield
        res[0] = dot3(operand(0), table(4))
        res[1] = dot3(operand(1), table(5))
        arrived()
        yield
        for first in range(0, width, CHUNK):
            here = slice(first, first + CHUNK)
            terms = []
            for side, span in enumerate((near, far)):
                er, ei = res[0, here, near], res[0, here, far]
                dr, di = res[1, here, near], res[1, here, far]
                if side == 0:
                    br, bi = er + dr, ei + di
                else:
                    br, bi = er - dr, ei - di
                pr, pi = probe_rot[0, here, span], probe_rot[1, here, span]
                wr, wi = win[0, here, span], win[1, here, span]
                terms.append((pr * br + pi * bi, pr * bi - pi * br))
                light_terms = (wr * br + wi * bi, wr * bi - wi * br)
                for part in (0, 1):
                    win[part, here, span] = light_terms[part]
                    if first == 0:
                        win[part, width : width + 8, span] = light_terms[part][:8]

            def take(part, at, count, piece, value):
                to = pl.ds(pl.multiple_of(col_base + piece * 128, 128), 128)
                span = pl.ds(pl.multiple_of(row_base + at, 8), count)
                new[part, span, to] = new[part, span, to] - value

            for part in (0, 1):
                left_term = terms[0][part]
                right_term = terms[1][part]
                pieces = (
                    jnp.where(lane, left_term, 0.0),
                    right_term,
                    jnp.where(lane, 0.0, left_term),
                )
                for piece, value in enumerate(pieces):
                    if first == 0:
                        take(part, 0, 8, piece, jnp.where(sub, value[:8], 0.0))
                        take(part, 8, CHUNK - 8, piece, value[8:])
                        take(part, width, 8, piece, jnp.where(sub, 0.0, value[:8]))
                    else:
                        take(part, first, CHUNK, piece, value)
        yield
        below = (first_rows < 8 - row_by)[None]
        lane_out = first_lanes < half - col_by
        row_back, col_back = lax.rem(8 - row_by, 8), lax.rem(half - col_by, half)
        for part in (0, 1):
            for first in range(0, width, CHUNK):
                sides = []
                for span in (near, far):
                    block8 = win[part, first : first + CHUNK + 8, span]
                    block8 = pltpu.roll(block8.reshape(-1, 8, half), row_back, 1)
                    block8 = jnp.where(below, block8[:-1], block8[1:]).reshape(CHUNK, half)
                    sides.append(pltpu.roll(block8, col_back, 1))
                here = slice(first, first + CHUNK)
                light_ref[part, here, near] += jnp.where(lane_out, sides[0], sides[1])
                light_ref[part, here, far] += jnp.where(lane_out, sides[1], sides[0])

    count = count_ref[0]

    def arrive():
        for load in waiting:
            load.wait()
        waiting.clear()

    def visit_some(group, carry, arrived=lambda: None):
        running = []
        for bank in range(TOGETHER):
            slot = group * TOGETHER + bank
            running.append(visit(jnp.minimum(slot, count - 1), slot < count, bank, arrived))
        step = 0
        while any(running):
            for bank, job in enumerate(running):
                if job is not None and step >= STAGGER * bank:
                    if next(job, "ended") == "ended":
                        running[bank] = None
            step += 1
        return carry

    visit_some(0, 0, arrive)
    lax.fori_loop(1, (count + TOGETHER - 1) // TOGETHER, visit_some, 0)
    core = new.at[:, half : half + rows, half : half + cols]
    pairs = [(new.at[:, at[0], at[1]], out) for at, out in zip(edges, sides_out)]
    pairs += [(core.at[:, at[0], at[1]], out) for at, out in zip(borders, sides_out[4:])]
    inside = (slice(half, rows - half), slice(half, cols - half))
    pairs.append((core.at[:, inside[0], inside[1]], tile_out.at[:, inside[0], inside[1]]))
    stores = [pltpu.make_async_copy(src, dst, out_sems.at[i]) for i, (src, dst) in enumerate(pairs)]
    for store in stores:
        store.start()
    per_part = width // 8
    for part in (0, 1):

        @pl.loop(0, per_part)
        def _(i):
            span = pl.ds(pl.multiple_of(i * 8, 8), 8)
            for side in (0, 1):
                lanes = slice(side * 128, (side + 1) * 128)
                light_out[(part * per_part + i) * 2 + side] = light_ref[part, span, lanes]

    for store in stores:
        store.wait()


def patterns(
    mesh_shape, counts, offsets, tables, order, probe, sums, measured, tile, frame, rims, rate
):
    width = probe.shape[1]
    half = width // 2
    rows, cols = tile.shape[1:]
    ext = (2, rows + width, cols + width)
    flat, tall = (2, half, cols + width), (2, rows, half)
    vmem = pl.BlockSpec(memory_space=pltpu.VMEM)
    smem = pl.BlockSpec(memory_space=pltpu.SMEM)
    hbm = pl.BlockSpec(memory_space=pl.ANY)
    stepped = len(sums) > 0
    units = 2 * width * width // 1024
    inner = (2, half, cols - width)
    outs = [tile.shape, flat, flat, tall, tall, tall, tall, inner, inner, (units, 8, 128)]
    return pl.pallas_call(
        functools.partial(patterns_kernel, mesh_shape, rate, stepped),
        in_specs=[smem] * 2
        + [vmem] * (3 + len(sums))
        + [hbm, pl.BlockSpec(memory_space=pltpu.HBM)]
        + [hbm] * (4 + len(frame)),
        out_specs=[pl.BlockSpec(memory_space=pltpu.HBM)] + [hbm] * 8 + [vmem],
        out_shape=[jax.ShapeDtypeStruct(shape, F32) for shape in outs],
        scratch_shapes=[
            pltpu.VMEM(ext, F32),
            pltpu.VMEM(ext, F32),
            pltpu.VMEM((2, measured.shape[0], width, half), F32),
            pltpu.VMEM((2, width + 8, width), F32),
            pltpu.VMEM(probe.shape, F32),
            pltpu.VMEM((TOGETHER,) + probe.shape, BF16),
            pltpu.VMEM((TOGETHER,) + probe.shape, BF16),
            pltpu.VMEM((TOGETHER,) + probe.shape, F32),
            pltpu.VMEM((TOGETHER, 2, width + 8, width), F32),
            pltpu.VMEM((TOGETHER,) + probe.shape, F32),
            pltpu.VMEM((TOGETHER, width, width), F32),
            pltpu.VMEM((TOGETHER, width, width), BF16),
            pltpu.VMEM((TOGETHER, width, width), BF16),
            pltpu.SemaphoreType.DMA((16,)),
            pltpu.SemaphoreType.DMA((9,)),
        ],
        compiler_params=pltpu.CompilerParams(vmem_limit_bytes=46 * MIB),
        name="patterns",
    )(counts, offsets, tables, order, probe, *sums, measured, tile, *frame, *rims)


MIDDLES = 4
LAST_STEPS = ("sum", "m0", "sum", "rows", "m1", "sum", "m2", "frame", "sum", "take_rows", "m3", "sum", "t0", "t1", "sum", "t2", "t3", "take_ends")
AGAIN_STEPS = ("sum", "rows", "m0", "m1", "m2", "sum", "m3", "frame", "sum", "take_rows", "t0", "sum", "t1", "take_ends", "sum", "t2", "corners", "sum", "t3")


class Exchange:
    def __init__(self, send_sems, recv_sems):
        self.sems = (send_sems, recv_sems)
        self.used = 0
        self.open = []

    def send(self, src, dst, to, landing=None):
        at = self.used
        self.used += 1
        copy = self.describe(src, dst, to, at)
        copy.start()
        arrival = copy if landing is None else self.describe(src, landing, to, at)
        self.open.append(copy)
        return arrival.wait_recv

    def describe(self, src, dst, to, at):
        return pltpu.make_async_remote_copy(
            src_ref=src,
            dst_ref=dst,
            send_sem=self.sems[0].at[at],
            recv_sem=self.sems[1].at[at],
            device_id=to,
            device_id_type=MESH,
        )

    def finish(self):
        for copy in self.open:
            copy.wait_send()


def greet(peers):
    barrier = pltpu.get_barrier_semaphore()
    for peer in peers:
        pl.semaphore_signal(barrier, inc=1, device_id=peer, device_id_type=MESH)
    pl.semaphore_wait(barrier, len(peers))


class Place:
    def __init__(self, mesh_shape):
        self.n_row, self.n_col = mesh_shape
        self.row = lax.axis_index("row")
        self.col = lax.axis_index("col")
        self.up = (lax.rem(self.row + self.n_row - 1, self.n_row), self.col)
        self.down = (lax.rem(self.row + 1, self.n_row), self.col)
        self.left = (self.row, lax.rem(self.col + self.n_col - 1, self.n_col))
        self.right = (self.row, lax.rem(self.col + 1, self.n_col))

    def near(self):
        return [self.up, self.down, self.left, self.right]

    def reducers(self):
        core = lax.rem(self.row, 2)
        partner = (self.row + 1 - 2 * core, self.col)
        along = [
            (lax.rem(self.row + 2 * j, self.n_row), self.col) for j in range(1, self.n_row // 2)
        ]
        across = [(self.row, lax.rem(self.col + j, self.n_col)) for j in range(1, self.n_col)]
        return partner, along, across


def probe_sum(place, net, light, total, first, second, got_core, got_row, got_col):
    partner, along, across = place.reducers()
    core, x = lax.rem(place.row, 2), lax.div(place.row, 2)
    n_x, n_col = place.n_row // 2, place.n_col
    big, mid = first.shape[0], second.shape[0]
    arrive = net.send(light.at[pl.ds((1 - core) * big, big)], got_core, partner)
    yield
    arrive()

    @pl.loop(0, big)
    def _(i):
        first[i] = light[core * big + i] + got_core[i]

    waits = []
    for j, peer in enumerate(along):
        there = lax.div(peer[0], 2)
        waits.append(net.send(first.at[pl.ds(there * mid, mid)], got_row.at[j], peer))
    yield
    for wait in waits:
        wait()

    @pl.loop(0, mid)
    def _(i):
        value = first[x * mid + i]
        for j in range(n_x - 1):
            value = value + got_row[j, i]
        second[i] = value

    waits = [net.send(second.at[peer[1]], got_col.at[j], peer) for j, peer in enumerate(across)]
    yield
    for wait in waits:
        wait()
    value = second[place.col]
    for j in range(n_col - 1):
        value = value + got_col[j]
    corner = core * big + x * mid
    mine = corner + place.col
    total[mine] = value
    waits = []
    for j, peer in enumerate(across):
        source = lax.rem(place.col + n_col - (j + 1), n_col)
        waits.append(net.send(total.at[mine], total.at[mine], peer, total.at[corner + source]))
    yield
    for wait in waits:
        wait()
    block = pl.ds(corner, mid)
    waits = []
    for j, peer in enumerate(along):
        source = lax.rem(x + n_x - (j + 1), n_x)
        landing = total.at[pl.ds(core * big + source * mid, mid)]
        waits.append(net.send(total.at[block], total.at[block], peer, landing))
    yield
    for wait in waits:
        wait()
    block = pl.ds(core * big, big)
    landing = total.at[pl.ds((1 - core) * big, big)]
    arrive = net.send(total.at[block], total.at[block], partner, landing)
    yield
    arrive()


def fetch_kernel(mesh_shape, half, tile, top, bottom, left, right, send_sems, recv_sems):
    place = Place(mesh_shape)
    net = Exchange(send_sems, recv_sems)
    rows, cols = tile.shape[1:]
    greet(place.near())
    ends = (slice(0, half), slice(rows - half, rows))
    first, last = slice(0, half), slice(cols - half, cols)
    inner = slice(half, half + cols)
    waits = []
    for end in ends:
        waits.append(net.send(tile.at[:, end, first], right.at[:, end], place.left))
        waits.append(net.send(tile.at[:, end, last], left.at[:, end], place.right))
    later = [
        net.send(tile.at[:, ends[0]], bottom.at[:, :, inner], place.up),
        net.send(tile.at[:, ends[1]], top.at[:, :, inner], place.down),
    ]
    middle = slice(half, rows - half)
    later.append(net.send(tile.at[:, middle, first], right.at[:, middle], place.left))
    later.append(net.send(tile.at[:, middle, last], left.at[:, middle], place.right))
    for wait in waits:
        wait()
    outer = (slice(0, half), slice(half + cols, 2 * half + cols))
    for rim, to in zip((left, right), outer):
        later.append(net.send(rim.at[:, ends[0]], bottom.at[:, :, to], place.up))
        later.append(net.send(rim.at[:, ends[1]], top.at[:, :, to], place.down))
    for wait in later:
        wait()
    net.finish()


def fetch_rims(mesh_shape, tile, half):
    rows, cols = tile.shape[1:]
    flat = jax.ShapeDtypeStruct((2, half, cols + 2 * half), F32)
    tall = jax.ShapeDtypeStruct((2, rows, half), F32)
    hbm = pl.BlockSpec(memory_space=pl.ANY)
    return pl.pallas_call(
        functools.partial(fetch_kernel, mesh_shape, half),
        in_specs=[pl.BlockSpec(memory_space=pltpu.HBM)],
        out_specs=[hbm] * 4,
        out_shape=[flat, flat, tall, tall],
        scratch_shapes=[pltpu.SemaphoreType.DMA((12,)), pltpu.SemaphoreType.DMA((12,))],
        compiler_params=pltpu.CompilerParams(
            collective_id=1, has_side_effects=True, vmem_limit_bytes=58 * MIB
        ),
        name="fetch_rims",
    )(tile)


def add_rows(target, at_rows, source, from_rows, from_cols):
    step = 32

    @pl.loop(0, at_rows.stop - at_rows.start, step=step)
    def _(i):
        to = pl.ds(pl.multiple_of(at_rows.start + i, step), step)
        here = pl.ds(pl.multiple_of(from_rows.start + i, step), step)
        target[:, to, :] = target[:, to, :] + source[:, here, from_cols]


def settle_kernel(mesh_shape, half, again, *refs):
    grad_top, grad_bottom, grad_left, grad_right, *border, light = refs[:9]
    refs = refs[9:]
    out_left, out_right, out_top, out_bottom, total_out = refs[:5]
    refs = refs[5:]
    if again:
        top, bottom, left, right = refs[:4]
        refs = refs[4:]
    (
        own_left,
        own_right,
        own_top,
        own_bottom,
        end_left,
        end_right,
        got_top,
        got_bottom,
        got_left,
        got_right,
        total,
        first_sum,
        second_sum,
        got_core,
        got_row,
        got_col,
        load_sems,
        send_sems,
        recv_sems,
    ) = refs
    place = Place(mesh_shape)
    net = Exchange(send_sems, recv_sems)
    rows, cols = grad_left.shape[1], grad_top.shape[2] - 2 * half
    partner, along, across = place.reducers()
    further = (lax.rem(place.row + place.n_row - 1 + 2 * lax.rem(place.row, 2), place.n_row), place.col)
    greet([partner, further] + along + across)

    up_end, down_end = slice(0, half), slice(rows - half, rows)
    whole = slice(0, half)
    wide = (slice(0, half), slice(half, 2 * half), slice(2 * half, cols), slice(cols, cols + half))
    wide = wide + (slice(cols + half, cols + 2 * half),)
    bounds = [half + i * (rows - 2 * half) // MIDDLES for i in range(MIDDLES + 1)]
    middles = [slice(i, j) for i, j in zip(bounds, bounds[1:])]
    pairs = (
        (grad_left.at[:, up_end], end_left.at[0]),
        (grad_left.at[:, down_end], end_left.at[1]),
        (grad_right.at[:, up_end], end_right.at[0]),
        (grad_right.at[:, down_end], end_right.at[1]),
    ) + tuple(zip(border, (own_left, own_right, own_top, own_bottom)))
    loads = [pltpu.make_async_copy(src, dst, load_sems.at[i]) for i, (src, dst) in enumerate(pairs)]
    for load in loads:
        load.start()
    sums = probe_sum(place, net, light, total, first_sum, second_sum, got_core, got_row, got_col)
    waits = {}

    def send_rows():
        waits["rows"] = [
            net.send(grad_top, got_bottom, place.up),
            net.send(grad_bottom, got_top, place.down),
        ]

    def send_middle(span):
        waits[span.start] = [
            net.send(grad_left.at[:, span], got_right.at[:, span], place.left),
            net.send(grad_right.at[:, span], got_left.at[:, span], place.right),
        ]

    def take_rows():
        for wait in waits["rows"]:
            wait()
        for end, (got, own, span, inside) in enumerate(
            (
                (got_top, own_top, up_end, place.row > 0),
                (got_bottom, own_bottom, down_end, place.row < place.n_row - 1),
            )
        ):

            @pl.when(inside)
            def _():
                add_rows(end_left.at[end], whole, got, whole, wide[0])
                add_rows(own_left, span, got, whole, wide[1])
                add_rows(own, whole, got, whole, wide[2])
                add_rows(own_right, span, got, whole, wide[3])
                add_rows(end_right.at[end], whole, got, whole, wide[4])

        waits["ends"] = []
        for end, span in enumerate((up_end, down_end)):
            waits["ends"].append(net.send(end_left.at[end], got_right.at[:, span], place.left))
            waits["ends"].append(net.send(end_right.at[end], got_left.at[:, span], place.right))

    def take_cols(span):
        @pl.when(place.col > 0)
        def _():
            add_rows(own_left, span, got_left, span, slice(None))

        @pl.when(place.col < place.n_col - 1)
        def _():
            add_rows(own_right, span, got_right, span, slice(None))

    def give_cols(span):
        return [
            net.send(own_left.at[:, span], right.at[:, span], place.left),
            net.send(own_right.at[:, span], left.at[:, span], place.right),
        ]

    later = []

    def take_middle(span):
        for wait in waits[span.start]:
            wait()
        take_cols(span)
        if again:
            later.extend(give_cols(span))

    def take_ends():
        for wait in waits["ends"]:
            wait()
        take_cols(up_end)
        take_cols(down_end)
        if again:
            waits["corners"] = give_cols(up_end) + give_cols(down_end)
            for span, own, rim, to in (
                (up_end, own_top, bottom, place.up),
                (down_end, own_bottom, top, place.down),
            ):
                later.append(net.send(own_left.at[:, span], rim.at[:, :, wide[1]], to))
                later.append(net.send(own, rim.at[:, :, wide[2]], to))
                later.append(net.send(own_right.at[:, span], rim.at[:, :, wide[3]], to))

    def send_corners():
        if again:
            for wait in waits["corners"]:
                wait()
            for rim, to in ((left, wide[0]), (right, wide[4])):
                later.append(net.send(rim.at[:, up_end], bottom.at[:, :, to], place.up))
                later.append(net.send(rim.at[:, down_end], top.at[:, :, to], place.down))

    def load_frame():
        for load in loads:
            load.wait()

    plain = {
        "rows": send_rows,
        "take_rows": take_rows,
        "take_ends": take_ends,
        "corners": send_corners,
        "frame": load_frame,
        "sum": lambda: next(sums, None),
    }
    for step in AGAIN_STEPS if again else LAST_STEPS:
        if step in plain:
            plain[step]()
        elif step[0] == "m":
            send_middle(middles[int(step[1:])])
        else:
            take_middle(middles[int(step[1:])])
    for _ in sums:
        pass
    stores = [
        pltpu.make_async_copy(src, dst, load_sems.at[i])
        for i, (src, dst) in enumerate(
            (
                (own_left, out_left),
                (own_right, out_right),
                (own_top, out_top),
                (own_bottom, out_bottom),
                (total, total_out),
            )
        )
    ]
    for store in stores:
        store.start()
    for wait in later:
        wait()
    net.finish()
    for store in stores:
        store.wait()


def settle(mesh_shape, strips, border, light, again):
    rows, half = strips[2].shape[1:]
    cols = strips[0].shape[2] - 2 * half
    n_row, n_col = mesh_shape
    big, mid = light.shape[0] // 2, light.shape[0] // n_row
    unit = light.shape[1:]
    flat, tall = (2, half, cols + 2 * half), (2, rows, half)
    inner, ends = (2, half, cols - 2 * half), (2, 2, half, half)
    outs = [tall, tall, inner, inner, light.shape] + ([flat, flat, tall, tall] if again else [])
    copies = 8 + 2 * MIDDLES + 2 * (n_col - 1) + 2 * (n_row // 2 - 1) + again * (14 + 2 * MIDDLES)
    hbm = pl.BlockSpec(memory_space=pl.ANY)
    vmem = pl.BlockSpec(memory_space=pltpu.VMEM)
    return pl.pallas_call(
        functools.partial(settle_kernel, mesh_shape, half, again),
        in_specs=[hbm] * 8 + [vmem],
        out_specs=[hbm] * len(outs),
        out_shape=[jax.ShapeDtypeStruct(shape, F32) for shape in outs],
        scratch_shapes=[
            pltpu.VMEM(tall, F32),
            pltpu.VMEM(tall, F32),
            pltpu.VMEM(inner, F32),
            pltpu.VMEM(inner, F32),
            pltpu.VMEM(ends, F32),
            pltpu.VMEM(ends, F32),
            pltpu.VMEM(flat, F32),
            pltpu.VMEM(flat, F32),
            pltpu.VMEM(tall, F32),
            pltpu.VMEM(tall, F32),
            pltpu.VMEM(light.shape, F32),
            pltpu.VMEM((big,) + unit, F32),
            pltpu.VMEM((mid,) + unit, F32),
            pltpu.VMEM((big,) + unit, F32),
            pltpu.VMEM((n_row // 2 - 1, mid) + unit, F32),
            pltpu.VMEM((n_col - 1,) + unit, F32),
            pltpu.SemaphoreType.DMA((8,)),
            pltpu.SemaphoreType.DMA((copies,)),
            pltpu.SemaphoreType.DMA((copies,)),
        ],
        compiler_params=pltpu.CompilerParams(
            collective_id=2 if again else 3, has_side_effects=True, vmem_limit_bytes=40 * MIB
        ),
        name="settle_and_fetch" if again else "settle",
    )(*strips, *border, light)


def finish_kernel(rate, *refs):
    probe, sum_first, sum_last, left, right, top, bottom, tile_in, tile, probe_out, sems = refs
    rows, cols = tile.shape[1:]
    half = left.shape[2]
    first, last, core_cols = slice(0, half), slice(cols - half, cols), slice(half, cols - half)
    pairs = (
        (left, tile.at[:, :, first]),
        (right, tile.at[:, :, last]),
        (top, tile.at[:, :half, core_cols]),
        (bottom, tile.at[:, rows - half :, core_cols]),
    )
    stores = [pltpu.make_async_copy(src, dst, sems.at[i]) for i, (src, dst) in enumerate(pairs)]
    for store in stores:
        store.start()
    step_probe(rate, probe, sum_first, probe_out)
    step_probe(rate, probe_out, sum_last, probe_out)
    for store in stores:
        store.wait()


def finish(probe, sums, frame, tile, rate):
    hbm = pl.BlockSpec(memory_space=pl.ANY)
    vmem = pl.BlockSpec(memory_space=pltpu.VMEM)
    return pl.pallas_call(
        functools.partial(finish_kernel, rate),
        in_specs=[vmem] * 7 + [hbm],
        out_specs=[hbm, vmem],
        out_shape=[
            jax.ShapeDtypeStruct(tile.shape, F32),
            jax.ShapeDtypeStruct(probe.shape, F32),
        ],
        scratch_shapes=[pltpu.SemaphoreType.DMA((4,))],
        input_output_aliases={7: 0},
        compiler_params=pltpu.CompilerParams(vmem_limit_bytes=40 * MIB),
        name="finish",
    )(probe, *sums, *frame, tile)


def step_probe(rate, probe, light, out, shift=0):
    width = probe.shape[1]
    per_part = width // 8
    for part in (0, 1):

        @pl.loop(0, per_part)
        def _(i):
            span = pl.ds(pl.multiple_of(i * 8, 8), 8)
            for side in (0, 1):
                lanes = slice(side * 128, (side + 1) * 128)
                block = light[(part * per_part + i) * 2 + side]
                to = pl.ds(pl.multiple_of(i * 8 + shift, 8), 8)
                out[part, to, lanes] = probe[part, span, lanes] - rate * block


def per_device(mesh_shape, object_field, illumination, measured, offsets, counts):
    width = illumination.shape[1]
    half = width // 2
    total = measured.shape[0] * mesh_shape[0] * mesh_shape[1]
    rate = LIGHT_RATE / total / OBJECT_RATE
    tables = jnp.asarray(factor_tables(width))
    order = jnp.asarray(parity_order(width))
    sums = []
    tile, frame, probe = object_field, (), illumination
    rims = fetch_rims(mesh_shape, tile, half)
    for sweep in range(ITERS):
        tile, *sides, light = patterns(
            mesh_shape, counts, offsets.T, tables, order, probe, sums, measured, tile, frame, rims, rate
        )
        found = settle(mesh_shape, sides[:4], sides[4:], light, sweep < ITERS - 1)
        frame, rims = found[:4], found[5:]
        sums.append(found[4])
    return finish(probe, sums, frame, tile, rate)


def solution(mesh):
    placed = (
        P(None, "row", "col"),
        P(),
        P(("row", "col"), None, None),
        P(("row", "col"), None),
        P(("row", "col")),
    )
    mesh_shape = (mesh.shape["row"], mesh.shape["col"])
    return jax.shard_map(
        functools.partial(per_device, mesh_shape),
        mesh=mesh,
        in_specs=placed,
        out_specs=(P(None, "row", "col"), P()),
        check_vma=False,
    )
```

```python
import functools
import math

import jax
import jax.numpy as jnp
import numpy as np
from jax import lax
from jax.experimental import pallas as pl
from jax.experimental.pallas import tpu as pltpu
from jax.sharding import PartitionSpec as P

ITERS = 2
OBJECT_RATE = 0.01
LIGHT_RATE = 0.02
MESH = pl.DeviceIdType.MESH
F32 = jnp.float32
BF16 = jnp.bfloat16
MIB = 1024 * 1024


def halves(array):
    high = array.astype(BF16)
    low = (array - high.astype(F32)).astype(BF16)
    return high, low


def factor_tables(length):
    half = length // 2
    index = np.arange(half)
    found = []
    for parity in (0, 1):
        phase = ((2 * index[:, None] + parity) * index[None, :]) % length
        angle = phase * (2.0 * math.pi / length)
        real = np.cos(angle) / math.sqrt(length)
        imag = -np.sin(angle) / math.sqrt(length)
        whole = np.block([[real, -imag], [imag, real]])
        found += [whole, whole.T]
    split = []
    for matrix in found + [OBJECT_RATE * found[0], OBJECT_RATE * found[2]]:
        matrix = matrix.astype(np.float32)
        high = matrix.astype(jnp.bfloat16)
        low = (matrix - high.astype(np.float32)).astype(jnp.bfloat16)
        split.append(np.stack([high, low]))
    return np.stack(split)


def parity_order(length):
    half = length // 2
    order = np.zeros((length, length), np.float32)
    order[2 * np.arange(half), np.arange(half)] = 1
    order[2 * np.arange(half) + 1, half + np.arange(half)] = 1
    return order.astype(jnp.bfloat16)


def dot(left, right):
    return jnp.dot(left, right, preferred_element_type=F32)


CHUNK = 32
STAGGER = 1
TOGETHER = 3


def margins(half, rows, cols):
    inner = slice(half, half + rows)
    return (
        (slice(0, half), slice(0, cols + 2 * half)),
        (slice(half + rows, rows + 2 * half), slice(0, cols + 2 * half)),
        (inner, slice(0, half)),
        (inner, slice(half + cols, cols + 2 * half)),
    )


def frame_parts(half, rows, cols):
    inner = slice(half, cols - half)
    return (
        (slice(0, rows), slice(0, half)),
        (slice(0, rows), slice(cols - half, cols)),
        (slice(0, half), inner),
        (slice(rows - half, rows), inner),
    )


def clear(ref, at_rows, at_cols):
    step = 8

    @pl.loop(at_rows.start, at_rows.stop, step=step)
    def _(i):
        at = pl.ds(pl.multiple_of(i, step), step)
        ref[:, at, at_cols] = jnp.zeros((2, step, at_cols.stop - at_cols.start), F32)


def patterns_kernel(mesh_shape, rate, stepped, *refs):
    count_ref, offset_ref, table_ref, order_ref, probe_in = refs[:5]
    refs = refs[5:]
    if stepped:
        light_in, refs = refs[0], refs[1:]
    measured_hbm, tile_hbm, refs = refs[0], refs[1], refs[2:]
    if stepped:
        frame, refs = refs[:4], refs[4:]
    rims, refs = refs[:4], refs[4:]
    tile_out, *sides_out, light_out = refs[:10]
    (
        ext,
        new,
        measured_ref,
        probe_now,
        *banks,
        in_sems,
        out_sems,
    ) = refs[10:]
    width = probe_in.shape[1]
    half = width // 2
    rows, cols = tile_hbm.shape[1:]
    edges = margins(half, rows, cols)
    borders = frame_parts(half, rows, cols)
    pairs = [(rim, ext.at[:, at[0], at[1]]) for rim, at in zip(rims, edges)]
    pairs += [
        (measured_hbm.at[:, :, side * half : (side + 1) * half], measured_ref.at[side])
        for side in (0, 1)
    ]
    for whole in (ext, new):
        core = whole.at[:, half : half + rows, half : half + cols]
        if stepped:
            core_rows, core_cols = slice(half, rows - half), slice(half, cols - half)
            pairs += [(part, core.at[:, at[0], at[1]]) for part, at in zip(frame, borders)]
            pairs.append((tile_hbm.at[:, core_rows, core_cols], core.at[:, core_rows, core_cols]))
        else:
            pairs.append((tile_hbm, core))
    loads = [pltpu.make_async_copy(src, dst, in_sems.at[i]) for i, (src, dst) in enumerate(pairs)]
    for load in loads:
        load.start()
    light_out[...] = jnp.zeros_like(light_out)
    for at in edges:
        clear(new, *at)
    probe_ref = probe_now
    if stepped:
        step_probe(rate, probe_in, light_in, probe_now, 8)
    else:
        probe_now[:, 8:, :] = probe_in[...]
    probe_now[:, :8, :] = probe_now[:, width:, :]
    split = 6 + (len(loads) - 6) // 2
    waiting = loads[split:]
    for load in loads[:split]:
        load.wait()
    all_rows = slice(0, rows + width)
    beyond = (edges[0], edges[1], (all_rows, edges[2][1]), (all_rows, edges[3][1]))
    row, col = lax.axis_index("row"), lax.axis_index("col")
    outside = (row == 0, row == mesh_shape[0] - 1, col == 0, col == mesh_shape[1] - 1)
    for i, at in enumerate(beyond):

        @pl.when(outside[i])
        def _():
            clear(ext, *at)

    def dot3(left, right):
        (lh, ll), (rh, rl) = left, right
        return dot(jnp.concatenate([lh, ll, lh], axis=1), jnp.concatenate([rh, rh, rl], axis=0))

    def table(which):
        return table_ref[which, 0], table_ref[which, 1]

    whole = slice(None)
    near, far = slice(0, half), slice(half, width)

    def visit(slot, live, bank, arrived):
        op_high, op_low, res, win, probe_rot, target = (ref.at[bank] for ref in banks)

        def put(which, at_rows, at_cols, value):
            high, low = halves(value)
            op_high[which, at_rows, at_cols] = high
            op_low[which, at_rows, at_cols] = low

        def operand(which):
            return op_high[which], op_low[which]

        row_at = offset_ref[0, slot]
        col_at = offset_ref[1, slot]
        row_base = pl.multiple_of((row_at // 8) * 8, 8)
        col_base = pl.multiple_of((col_at // 128) * 128, 128)
        row_by = row_at - row_base
        col_by = col_at - col_base
        first_lanes = lax.broadcasted_iota(jnp.int32, (CHUNK, half), 1)
        first_rows = lax.broadcasted_iota(jnp.int32, (8, half), 0)
        lane = first_lanes >= col_by
        sub = first_rows >= row_by

        def block(ref, part, first, count, piece):
            at = pl.multiple_of(col_base + piece * 128, 128)
            return ref[part, pl.ds(pl.multiple_of(row_base + first, 8), count), pl.ds(at, 128)]

        for parity, to in enumerate((near, far)):
            picked = pl.ds(parity, half, stride=2)
            for side, span in enumerate((near, far)):
                put(0, to, span, measured_ref[side, slot, picked, :])
        yield
        target[...] = dot(op_high[0], order_ref[...]) + dot(op_low[0], order_ref[...])
        above = (first_rows >= row_by)[None]
        lane_in = first_lanes >= col_by
        for part in (0, 1):
            for first in range(0, width, CHUNK):
                sides = []
                for span in (near, far):
                    block8 = probe_ref[part, first : first + CHUNK + 8, span]
                    block8 = pltpu.roll(block8.reshape(-1, 8, half), row_by, 1)
                    block8 = jnp.where(above, block8[1:], block8[:-1]).reshape(CHUNK, half)
                    sides.append(pltpu.roll(block8, col_by, 1))
                here = slice(first, first + CHUNK)
                probe_rot[part, here, near] = jnp.where(lane_in, sides[0], sides[1])
                probe_rot[part, here, far] = jnp.where(lane_in, sides[1], sides[0])
        yield
        for first in range(0, width, CHUNK):
            here = slice(first, first + CHUNK)
            fields = []
            for part in (0, 1):
                pieces = []
                for piece in range(3):
                    body = block(ext, part, first, CHUNK, piece)
                    if first == 0:
                        tail = block(ext, part, width, 8, piece)
                        body = jnp.concatenate([jnp.where(sub, body[:8], tail), body[8:]], axis=0)
                    pieces.append(body)
                near_cols = jnp.where(lane, pieces[0], pieces[2])
                fields.append((near_cols, pieces[1]))
                win[part, here, near] = near_cols
                win[part, here, far] = pieces[1]
            exits = []
            for side, span in enumerate((near, far)):
                wr, wi = fields[0][side], fields[1][side]
                pr, pi = probe_rot[0, here, span], probe_rot[1, here, span]
                exits.append((pr * wr - pi * wi, pr * wi + pi * wr))
            for part, span in enumerate((near, far)):
                put(0, here, span, exits[0][part] + exits[1][part])
                put(1, here, span, exits[0][part] - exits[1][part])
        yield
        res[0] = dot3(operand(0), table(1))
        res[1] = dot3(operand(1), table(3))
        yield
        for part, rows_to in enumerate((near, far)):
            for parity, cols_to in enumerate((near, far)):
                upper = res[parity, near, rows_to]
                lower = res[parity, far, rows_to]
                put(0, rows_to, cols_to, upper + lower)
                put(1, rows_to, cols_to, upper - lower)
        yield
        res[0] = dot3(table(0), operand(0))
        res[1] = dot3(table(2), operand(1))
        yield
        for parity in (0, 1):
            re, im = res[parity, near, :], res[parity, far, :]
            rows_from = slice(parity * half, (parity + 1) * half)
            misfit = re * re + im * im - target[rows_from, :]
            misfit = jnp.where(live, misfit, 0.0)
            put(parity, near, whole, misfit * re)
            put(parity, far, whole, misfit * im)
        yield
        res[0] = dot3(table(1), operand(0))
        res[1] = dot3(table(3), operand(1))
        yield
        for part, cols_to in enumerate((near, far)):
            for parity, cols_from in enumerate((near, far)):
                first = res[0, cols_to, cols_from]
                second = res[1, cols_to, cols_from]
                put(parity, near, cols_to, first + second)
                put(parity, far, cols_to, first - second)
        yield
        res[0] = dot3(operand(0), table(4))
        res[1] = dot3(operand(1), table(5))
        arrived()
        yield
        for first in range(0, width, CHUNK):
            here = slice(first, first + CHUNK)
            terms = []
            for side, span in enumerate((near, far)):
                er, ei = res[0, here, near], res[0, here, far]
                dr, di = res[1, here, near], res[1, here, far]
                if side == 0:
                    br, bi = er + dr, ei + di
                else:
                    br, bi = er - dr, ei - di
                pr, pi = probe_rot[0, here, span], probe_rot[1, here, span]
                wr, wi = win[0, here, span], win[1, here, span]
                terms.append((pr * br + pi * bi, pr * bi - pi * br))
                light_terms = (wr * br + wi * bi, wr * bi - wi * br)
                for part in (0, 1):
                    win[part, here, span] = light_terms[part]
                    if first == 0:
                        win[part, width : width + 8, span] = light_terms[part][:8]

            def take(part, at, count, piece, value):
                to = pl.ds(pl.multiple_of(col_base + piece * 128, 128), 128)
                span = pl.ds(pl.multiple_of(row_base + at, 8), count)
                new[part, span, to] = new[part, span, to] - value

            for part in (0, 1):
                left_term = terms[0][part]
                right_term = terms[1][part]
                pieces = (
                    jnp.where(lane, left_term, 0.0),
                    right_term,
                    jnp.where(lane, 0.0, left_term),
                )
                for piece, value in enumerate(pieces):
                    if first == 0:
                        take(part, 0, 8, piece, jnp.where(sub, value[:8], 0.0))
                        take(part, 8, CHUNK - 8, piece, value[8:])
                        take(part, width, 8, piece, jnp.where(sub, 0.0, value[:8]))
                    else:
                        take(part, first, CHUNK, piece, value)
        yield
        below = (first_rows < 8 - row_by)[None]
        lane_out = first_lanes < half - col_by
        row_back, col_back = lax.rem(8 - row_by, 8), lax.rem(half - col_by, half)
        for part in (0, 1):
            for first in range(0, width, CHUNK):
                sides = []
                for span in (near, far):
                    block8 = win[part, first : first + CHUNK + 8, span]
                    block8 = pltpu.roll(block8.reshape(-1, 8, half), row_back, 1)
                    block8 = jnp.where(below, block8[:-1], block8[1:]).reshape(CHUNK, half)
                    sides.append(pltpu.roll(block8, col_back, 1))
                turned = (
                    jnp.where(lane_out, sides[0], sides[1]),
                    jnp.where(lane_out, sides[1], sides[0]),
                )
                for i in range(CHUNK // 8):
                    unit = (part * (width // 8) + first // 8 + i) * 2
                    for side in (0, 1):
                        light_out[unit + side] += turned[side][8 * i : 8 * i + 8]

    count = count_ref[0]

    def arrive():
        for load in waiting:
            load.wait()
        waiting.clear()

    def visit_some(group, carry, arrived=lambda: None):
        running = []
        for bank in range(TOGETHER):
            slot = group * TOGETHER + bank
            running.append(visit(jnp.minimum(slot, count - 1), slot < count, bank, arrived))
        step = 0
        while any(running):
            for bank, job in enumerate(running):
                if job is not None and step >= STAGGER * bank:
                    if next(job, "ended") == "ended":
                        running[bank] = None
            step += 1
        return carry

    visit_some(0, 0, arrive)
    lax.fori_loop(1, (count + TOGETHER - 1) // TOGETHER, visit_some, 0)
    core = new.at[:, half : half + rows, half : half + cols]
    pairs = [(new.at[:, at[0], at[1]], out) for at, out in zip(edges, sides_out)]
    pairs += [(core.at[:, at[0], at[1]], out) for at, out in zip(borders, sides_out[4:])]
    inside = (slice(half, rows - half), slice(half, cols - half))
    pairs.append((core.at[:, inside[0], inside[1]], tile_out.at[:, inside[0], inside[1]]))
    stores = [pltpu.make_async_copy(src, dst, out_sems.at[i]) for i, (src, dst) in enumerate(pairs)]
    for store in stores:
        store.start()
    for store in stores:
        store.wait()


def patterns(
    mesh_shape, counts, offsets, tables, order, probe, sums, measured, tile, frame, rims, rate
):
    width = probe.shape[1]
    half = width // 2
    rows, cols = tile.shape[1:]
    ext = (2, rows + width, cols + width)
    flat, tall = (2, half, cols + width), (2, rows, half)
    vmem = pl.BlockSpec(memory_space=pltpu.VMEM)
    smem = pl.BlockSpec(memory_space=pltpu.SMEM)
    hbm = pl.BlockSpec(memory_space=pl.ANY)
    stepped = len(sums) > 0
    units = 2 * width * width // 1024
    inner = (2, half, cols - width)
    outs = [tile.shape, flat, flat, tall, tall, tall, tall, inner, inner, (units, 8, 128)]
    return pl.pallas_call(
        functools.partial(patterns_kernel, mesh_shape, rate, stepped),
        in_specs=[smem] * 2
        + [vmem] * (3 + len(sums))
        + [hbm, pl.BlockSpec(memory_space=pltpu.HBM)]
        + [hbm] * (4 + len(frame)),
        out_specs=[pl.BlockSpec(memory_space=pltpu.HBM)] + [hbm] * 8 + [vmem],
        out_shape=[jax.ShapeDtypeStruct(shape, F32) for shape in outs],
        scratch_shapes=[
            pltpu.VMEM(ext, F32),
            pltpu.VMEM(ext, F32),
            pltpu.VMEM((2, measured.shape[0], width, half), F32),
            pltpu.VMEM((2, width + 8, width), F32),
            pltpu.VMEM((TOGETHER,) + probe.shape, BF16),
            pltpu.VMEM((TOGETHER,) + probe.shape, BF16),
            pltpu.VMEM((TOGETHER,) + probe.shape, F32),
            pltpu.VMEM((TOGETHER, 2, width + 8, width), F32),
            pltpu.VMEM((TOGETHER,) + probe.shape, F32),
            pltpu.VMEM((TOGETHER, width, width), F32),
            pltpu.SemaphoreType.DMA((16,)),
            pltpu.SemaphoreType.DMA((9,)),
        ],
        compiler_params=pltpu.CompilerParams(vmem_limit_bytes=(35 if stepped else 35) * MIB),
        name="patterns",
    )(counts, offsets, tables, order, probe, *sums, measured, tile, *frame, *rims)


MIDDLES = 4
LAST_STEPS = ("sum", "m0", "sum", "rows", "m1", "sum", "m2", "frame", "sum", "take_rows", "m3", "sum", "t0", "t1", "sum", "t2", "t3", "take_ends")
AGAIN_STEPS = ("sum", "rows", "m0", "m1", "m2", "sum", "m3", "frame", "sum", "take_rows", "t0", "sum", "t1", "take_ends", "sum", "t2", "corners", "sum", "t3")


class Exchange:
    def __init__(self, send_sems, recv_sems):
        self.sems = (send_sems, recv_sems)
        self.used = 0
        self.open = []

    def send(self, src, dst, to, landing=None):
        at = self.used
        self.used += 1
        copy = self.describe(src, dst, to, at)
        copy.start()
        arrival = copy if landing is None else self.describe(src, landing, to, at)
        self.open.append(copy)
        return arrival.wait_recv

    def describe(self, src, dst, to, at):
        return pltpu.make_async_remote_copy(
            src_ref=src,
            dst_ref=dst,
            send_sem=self.sems[0].at[at],
            recv_sem=self.sems[1].at[at],
            device_id=to,
            device_id_type=MESH,
        )

    def finish(self):
        for copy in self.open:
            copy.wait_send()


def greet(peers):
    barrier = pltpu.get_barrier_semaphore()
    for peer in peers:
        pl.semaphore_signal(barrier, inc=1, device_id=peer, device_id_type=MESH)
    pl.semaphore_wait(barrier, len(peers))


class Place:
    def __init__(self, mesh_shape):
        self.n_row, self.n_col = mesh_shape
        self.row = lax.axis_index("row")
        self.col = lax.axis_index("col")
        self.up = (lax.rem(self.row + self.n_row - 1, self.n_row), self.col)
        self.down = (lax.rem(self.row + 1, self.n_row), self.col)
        self.left = (self.row, lax.rem(self.col + self.n_col - 1, self.n_col))
        self.right = (self.row, lax.rem(self.col + 1, self.n_col))

    def near(self):
        return [self.up, self.down, self.left, self.right]

    def reducers(self):
        core = lax.rem(self.row, 2)
        partner = (self.row + 1 - 2 * core, self.col)
        along = [
            (lax.rem(self.row + 2 * j, self.n_row), self.col) for j in range(1, self.n_row // 2)
        ]
        across = [(self.row, lax.rem(self.col + j, self.n_col)) for j in range(1, self.n_col)]
        return partner, along, across


def probe_sum(place, net, light, total, first, second, got_core, got_row, got_col):
    partner, along, across = place.reducers()
    core, x = lax.rem(place.row, 2), lax.div(place.row, 2)
    n_x, n_col = place.n_row // 2, place.n_col
    big, mid = first.shape[0], second.shape[0]
    arrive = net.send(light.at[pl.ds((1 - core) * big, big)], got_core, partner)
    yield
    arrive()

    @pl.loop(0, big)
    def _(i):
        first[i] = light[core * big + i] + got_core[i]

    waits = []
    for j, peer in enumerate(along):
        there = lax.div(peer[0], 2)
        waits.append(net.send(first.at[pl.ds(there * mid, mid)], got_row.at[j], peer))
    yield
    for wait in waits:
        wait()

    @pl.loop(0, mid)
    def _(i):
        value = first[x * mid + i]
        for j in range(n_x - 1):
            value = value + got_row[j, i]
        second[i] = value

    waits = [net.send(second.at[peer[1]], got_col.at[j], peer) for j, peer in enumerate(across)]
    yield
    for wait in waits:
        wait()
    value = second[place.col]
    for j in range(n_col - 1):
        value = value + got_col[j]
    corner = core * big + x * mid
    mine = corner + place.col
    total[mine] = value
    waits = []
    for j, peer in enumerate(across):
        source = lax.rem(place.col + n_col - (j + 1), n_col)
        waits.append(net.send(total.at[mine], total.at[mine], peer, total.at[corner + source]))
    yield
    for wait in waits:
        wait()
    block = pl.ds(corner, mid)
    waits = []
    for j, peer in enumerate(along):
        source = lax.rem(x + n_x - (j + 1), n_x)
        landing = total.at[pl.ds(core * big + source * mid, mid)]
        waits.append(net.send(total.at[block], total.at[block], peer, landing))
    yield
    for wait in waits:
        wait()
    block = pl.ds(core * big, big)
    landing = total.at[pl.ds((1 - core) * big, big)]
    arrive = net.send(total.at[block], total.at[block], partner, landing)
    yield
    arrive()


def fetch_kernel(mesh_shape, half, tile, top, bottom, left, right, send_sems, recv_sems):
    place = Place(mesh_shape)
    net = Exchange(send_sems, recv_sems)
    rows, cols = tile.shape[1:]
    greet(place.near())
    ends = (slice(0, half), slice(rows - half, rows))
    first, last = slice(0, half), slice(cols - half, cols)
    inner = slice(half, half + cols)
    waits = []
    for end in ends:
        waits.append(net.send(tile.at[:, end, first], right.at[:, end], place.left))
        waits.append(net.send(tile.at[:, end, last], left.at[:, end], place.right))
    later = [
        net.send(tile.at[:, ends[0]], bottom.at[:, :, inner], place.up),
        net.send(tile.at[:, ends[1]], top.at[:, :, inner], place.down),
    ]
    middle = slice(half, rows - half)
    later.append(net.send(tile.at[:, middle, first], right.at[:, middle], place.left))
    later.append(net.send(tile.at[:, middle, last], left.at[:, middle], place.right))
    for wait in waits:
        wait()
    outer = (slice(0, half), slice(half + cols, 2 * half + cols))
    for rim, to in zip((left, right), outer):
        later.append(net.send(rim.at[:, ends[0]], bottom.at[:, :, to], place.up))
        later.append(net.send(rim.at[:, ends[1]], top.at[:, :, to], place.down))
    for wait in later:
        wait()
    net.finish()


def fetch_rims(mesh_shape, tile, half):
    rows, cols = tile.shape[1:]
    flat = jax.ShapeDtypeStruct((2, half, cols + 2 * half), F32)
    tall = jax.ShapeDtypeStruct((2, rows, half), F32)
    hbm = pl.BlockSpec(memory_space=pl.ANY)
    return pl.pallas_call(
        functools.partial(fetch_kernel, mesh_shape, half),
        in_specs=[pl.BlockSpec(memory_space=pltpu.HBM)],
        out_specs=[hbm] * 4,
        out_shape=[flat, flat, tall, tall],
        scratch_shapes=[pltpu.SemaphoreType.DMA((12,)), pltpu.SemaphoreType.DMA((12,))],
        compiler_params=pltpu.CompilerParams(
            collective_id=1, has_side_effects=True, vmem_limit_bytes=49 * MIB
        ),
        name="fetch_rims",
    )(tile)


def add_rows(target, at_rows, source, from_rows, from_cols):
    step = 32

    @pl.loop(0, at_rows.stop - at_rows.start, step=step)
    def _(i):
        to = pl.ds(pl.multiple_of(at_rows.start + i, step), step)
        here = pl.ds(pl.multiple_of(from_rows.start + i, step), step)
        target[:, to, :] = target[:, to, :] + source[:, here, from_cols]


def settle_kernel(mesh_shape, half, again, *refs):
    grad_top, grad_bottom, grad_left, grad_right, *border, light = refs[:9]
    refs = refs[9:]
    out_left, out_right, out_top, out_bottom, total_out = refs[:5]
    refs = refs[5:]
    if again:
        top, bottom, left, right = refs[:4]
        refs = refs[4:]
    (
        own_left,
        own_right,
        own_top,
        own_bottom,
        end_left,
        end_right,
        got_top,
        got_bottom,
        got_left,
        got_right,
        total,
        first_sum,
        second_sum,
        got_core,
        got_row,
        got_col,
        load_sems,
        send_sems,
        recv_sems,
    ) = refs
    place = Place(mesh_shape)
    net = Exchange(send_sems, recv_sems)
    rows, cols = grad_left.shape[1], grad_top.shape[2] - 2 * half
    partner, along, across = place.reducers()
    further = (lax.rem(place.row + place.n_row - 1 + 2 * lax.rem(place.row, 2), place.n_row), place.col)
    greet([partner, further] + along + across)

    up_end, down_end = slice(0, half), slice(rows - half, rows)
    whole = slice(0, half)
    wide = (slice(0, half), slice(half, 2 * half), slice(2 * half, cols), slice(cols, cols + half))
    wide = wide + (slice(cols + half, cols + 2 * half),)
    bounds = [half + i * (rows - 2 * half) // MIDDLES for i in range(MIDDLES + 1)]
    middles = [slice(i, j) for i, j in zip(bounds, bounds[1:])]
    pairs = (
        (grad_left.at[:, up_end], end_left.at[0]),
        (grad_left.at[:, down_end], end_left.at[1]),
        (grad_right.at[:, up_end], end_right.at[0]),
        (grad_right.at[:, down_end], end_right.at[1]),
    ) + tuple(zip(border, (own_left, own_right, own_top, own_bottom)))
    loads = [pltpu.make_async_copy(src, dst, load_sems.at[i]) for i, (src, dst) in enumerate(pairs)]
    for load in loads:
        load.start()
    sums = probe_sum(place, net, light, total, first_sum, second_sum, got_core, got_row, got_col)
    waits = {}

    def send_rows():
        waits["rows"] = [
            net.send(grad_top, got_bottom, place.up),
            net.send(grad_bottom, got_top, place.down),
        ]

    def send_middle(span):
        waits[span.start] = [
            net.send(grad_left.at[:, span], got_right.at[:, span], place.left),
            net.send(grad_right.at[:, span], got_left.at[:, span], place.right),
        ]

    def take_rows():
        for wait in waits["rows"]:
            wait()
        for end, (got, own, span, inside) in enumerate(
            (
                (got_top, own_top, up_end, place.row > 0),
                (got_bottom, own_bottom, down_end, place.row < place.n_row - 1),
            )
        ):

            @pl.when(inside)
            def _():
                add_rows(end_left.at[end], whole, got, whole, wide[0])
                add_rows(own_left, span, got, whole, wide[1])
                add_rows(own, whole, got, whole, wide[2])
                add_rows(own_right, span, got, whole, wide[3])
                add_rows(end_right.at[end], whole, got, whole, wide[4])

        waits["ends"] = []
        for end, span in enumerate((up_end, down_end)):
            waits["ends"].append(net.send(end_left.at[end], got_right.at[:, span], place.left))
            waits["ends"].append(net.send(end_right.at[end], got_left.at[:, span], place.right))

    def take_cols(span):
        @pl.when(place.col > 0)
        def _():
            add_rows(own_left, span, got_left, span, slice(None))

        @pl.when(place.col < place.n_col - 1)
        def _():
            add_rows(own_right, span, got_right, span, slice(None))

    def give_cols(span):
        return [
            net.send(own_left.at[:, span], right.at[:, span], place.left),
            net.send(own_right.at[:, span], left.at[:, span], place.right),
        ]

    later = []

    def take_middle(span):
        for wait in waits[span.start]:
            wait()
        take_cols(span)
        if again:
            later.extend(give_cols(span))

    def take_ends():
        for wait in waits["ends"]:
            wait()
        take_cols(up_end)
        take_cols(down_end)
        if again:
            waits["corners"] = give_cols(up_end) + give_cols(down_end)
            for span, own, rim, to in (
                (up_end, own_top, bottom, place.up),
                (down_end, own_bottom, top, place.down),
            ):
                later.append(net.send(own_left.at[:, span], rim.at[:, :, wide[1]], to))
                later.append(net.send(own, rim.at[:, :, wide[2]], to))
                later.append(net.send(own_right.at[:, span], rim.at[:, :, wide[3]], to))

    def send_corners():
        if again:
            for wait in waits["corners"]:
                wait()
            for rim, to in ((left, wide[0]), (right, wide[4])):
                later.append(net.send(rim.at[:, up_end], bottom.at[:, :, to], place.up))
                later.append(net.send(rim.at[:, down_end], top.at[:, :, to], place.down))

    def load_frame():
        for load in loads:
            load.wait()

    plain = {
        "rows": send_rows,
        "take_rows": take_rows,
        "take_ends": take_ends,
        "corners": send_corners,
        "frame": load_frame,
        "sum": lambda: next(sums, None),
    }
    for step in AGAIN_STEPS if again else LAST_STEPS:
        if step in plain:
            plain[step]()
        elif step[0] == "m":
            send_middle(middles[int(step[1:])])
        else:
            take_middle(middles[int(step[1:])])
    for _ in sums:
        pass
    stores = [
        pltpu.make_async_copy(src, dst, load_sems.at[i])
        for i, (src, dst) in enumerate(
            (
                (own_left, out_left),
                (own_right, out_right),
                (own_top, out_top),
                (own_bottom, out_bottom),
                (total, total_out),
            )
        )
    ]
    for store in stores:
        store.start()
    for wait in later:
        wait()
    net.finish()
    for store in stores:
        store.wait()


def settle(mesh_shape, strips, border, light, again):
    rows, half = strips[2].shape[1:]
    cols = strips[0].shape[2] - 2 * half
    n_row, n_col = mesh_shape
    big, mid = light.shape[0] // 2, light.shape[0] // n_row
    unit = light.shape[1:]
    flat, tall = (2, half, cols + 2 * half), (2, rows, half)
    inner, ends = (2, half, cols - 2 * half), (2, 2, half, half)
    outs = [tall, tall, inner, inner, light.shape] + ([flat, flat, tall, tall] if again else [])
    copies = 8 + 2 * MIDDLES + 2 * (n_col - 1) + 2 * (n_row // 2 - 1) + again * (14 + 2 * MIDDLES)
    hbm = pl.BlockSpec(memory_space=pl.ANY)
    vmem = pl.BlockSpec(memory_space=pltpu.VMEM)
    return pl.pallas_call(
        functools.partial(settle_kernel, mesh_shape, half, again),
        in_specs=[hbm] * 8 + [vmem],
        out_specs=[hbm] * len(outs),
        out_shape=[jax.ShapeDtypeStruct(shape, F32) for shape in outs],
        scratch_shapes=[
            pltpu.VMEM(tall, F32),
            pltpu.VMEM(tall, F32),
            pltpu.VMEM(inner, F32),
            pltpu.VMEM(inner, F32),
            pltpu.VMEM(ends, F32),
            pltpu.VMEM(ends, F32),
            pltpu.VMEM(flat, F32),
            pltpu.VMEM(flat, F32),
            pltpu.VMEM(tall, F32),
            pltpu.VMEM(tall, F32),
            pltpu.VMEM(light.shape, F32),
            pltpu.VMEM((big,) + unit, F32),
            pltpu.VMEM((mid,) + unit, F32),
            pltpu.VMEM((big,) + unit, F32),
            pltpu.VMEM((n_row // 2 - 1, mid) + unit, F32),
            pltpu.VMEM((n_col - 1,) + unit, F32),
            pltpu.SemaphoreType.DMA((8,)),
            pltpu.SemaphoreType.DMA((copies,)),
            pltpu.SemaphoreType.DMA((copies,)),
        ],
        compiler_params=pltpu.CompilerParams(
            collective_id=2 if again else 3, has_side_effects=True, vmem_limit_bytes=20 * MIB
        ),
        name="settle_and_fetch" if again else "settle",
    )(*strips, *border, light)


def finish_kernel(rate, *refs):
    probe, sum_first, sum_last, left, right, top, bottom, tile_in, tile, probe_out, sems = refs
    rows, cols = tile.shape[1:]
    half = left.shape[2]
    first, last, core_cols = slice(0, half), slice(cols - half, cols), slice(half, cols - half)
    pairs = (
        (left, tile.at[:, :, first]),
        (right, tile.at[:, :, last]),
        (top, tile.at[:, :half, core_cols]),
        (bottom, tile.at[:, rows - half :, core_cols]),
    )
    stores = [pltpu.make_async_copy(src, dst, sems.at[i]) for i, (src, dst) in enumerate(pairs)]
    for store in stores:
        store.start()
    step_probe(rate, probe, sum_first, probe_out)
    step_probe(rate, probe_out, sum_last, probe_out)
    for store in stores:
        store.wait()


def finish(probe, sums, frame, tile, rate):
    hbm = pl.BlockSpec(memory_space=pl.ANY)
    vmem = pl.BlockSpec(memory_space=pltpu.VMEM)
    return pl.pallas_call(
        functools.partial(finish_kernel, rate),
        in_specs=[vmem] * 7 + [hbm],
        out_specs=[hbm, vmem],
        out_shape=[
            jax.ShapeDtypeStruct(tile.shape, F32),
            jax.ShapeDtypeStruct(probe.shape, F32),
        ],
        scratch_shapes=[pltpu.SemaphoreType.DMA((4,))],
        input_output_aliases={7: 0},
        compiler_params=pltpu.CompilerParams(vmem_limit_bytes=40 * MIB),
        name="finish",
    )(probe, *sums, *frame, tile)


def step_probe(rate, probe, light, out, shift=0):
    width = probe.shape[1]
    per_part = width // 8
    for part in (0, 1):

        @pl.loop(0, per_part)
        def _(i):
            span = pl.ds(pl.multiple_of(i * 8, 8), 8)
            for side in (0, 1):
                lanes = slice(side * 128, (side + 1) * 128)
                block = light[(part * per_part + i) * 2 + side]
                to = pl.ds(pl.multiple_of(i * 8 + shift, 8), 8)
                out[part, to, lanes] = probe[part, span, lanes] - rate * block


def per_device(mesh_shape, object_field, illumination, measured, offsets, counts):
    width = illumination.shape[1]
    half = width // 2
    total = measured.shape[0] * mesh_shape[0] * mesh_shape[1]
    rate = LIGHT_RATE / total / OBJECT_RATE
    tables = jnp.asarray(factor_tables(width))
    order = jnp.asarray(parity_order(width))
    sums = []
    tile, frame, probe = object_field, (), illumination
    rims = fetch_rims(mesh_shape, tile, half)
    for sweep in range(ITERS):
        tile, *sides, light = patterns(
            mesh_shape, counts, offsets.T, tables, order, probe, sums, measured, tile, frame, rims, rate
        )
        found = settle(mesh_shape, sides[:4], sides[4:], light, sweep < ITERS - 1)
        frame, rims = found[:4], found[5:]
        sums.append(found[4])
    return finish(probe, sums, frame, tile, rate)


def solution(mesh):
    placed = (
        P(None, "row", "col"),
        P(),
        P(("row", "col"), None, None),
        P(("row", "col"), None),
        P(("row", "col")),
    )
    mesh_shape = (mesh.shape["row"], mesh.shape["col"])
    return jax.shard_map(
        functools.partial(per_device, mesh_shape),
        mesh=mesh,
        in_specs=placed,
        out_specs=(P(None, "row", "col"), P()),
        check_vma=False,
    )
```

```python
import functools
import math

import jax
import jax.numpy as jnp
import numpy as np
from jax import lax
from jax.experimental import pallas as pl
from jax.experimental.pallas import tpu as pltpu
from jax.sharding import PartitionSpec as P

ITERS = 2
OBJECT_RATE = 0.01
LIGHT_RATE = 0.02
MESH = pl.DeviceIdType.MESH
F32 = jnp.float32
BF16 = jnp.bfloat16
MIB = 1024 * 1024


def halves(array):
    high = array.astype(BF16)
    low = (array - high.astype(F32)).astype(BF16)
    return high, low


def factor_tables(length):
    half = length // 2
    index = np.arange(half)
    found = []
    for parity in (0, 1):
        phase = ((2 * index[:, None] + parity) * index[None, :]) % length
        angle = phase * (2.0 * math.pi / length)
        real = np.cos(angle) / math.sqrt(length)
        imag = -np.sin(angle) / math.sqrt(length)
        whole = np.block([[real, -imag], [imag, real]])
        found += [whole, whole.T]
    split = []
    for matrix in found + [OBJECT_RATE * found[0], OBJECT_RATE * found[2]]:
        matrix = matrix.astype(np.float32)
        high = matrix.astype(jnp.bfloat16)
        low = (matrix - high.astype(np.float32)).astype(jnp.bfloat16)
        split.append(np.stack([high, low]))
    return np.stack(split)


def parity_order(length):
    half = length // 2
    order = np.zeros((length, length), np.float32)
    order[2 * np.arange(half), np.arange(half)] = 1
    order[2 * np.arange(half) + 1, half + np.arange(half)] = 1
    return order.astype(jnp.bfloat16)


def dot(left, right):
    return jnp.dot(left, right, preferred_element_type=F32)


CHUNK = 32
STAGGER = 1
TOGETHER = 3


def margins(half, rows, cols):
    inner = slice(half, half + rows)
    return (
        (slice(0, half), slice(0, cols + 2 * half)),
        (slice(half + rows, rows + 2 * half), slice(0, cols + 2 * half)),
        (inner, slice(0, half)),
        (inner, slice(half + cols, cols + 2 * half)),
    )


def frame_parts(half, rows, cols):
    inner = slice(half, cols - half)
    return (
        (slice(0, rows), slice(0, half)),
        (slice(0, rows), slice(cols - half, cols)),
        (slice(0, half), inner),
        (slice(rows - half, rows), inner),
    )


def clear(ref, at_rows, at_cols):
    step = 8

    @pl.loop(at_rows.start, at_rows.stop, step=step)
    def _(i):
        at = pl.ds(pl.multiple_of(i, step), step)
        ref[:, at, at_cols] = jnp.zeros((2, step, at_cols.stop - at_cols.start), F32)


def patterns_kernel(mesh_shape, rate, stepped, *refs):
    count_ref, offset_ref, table_ref, order_ref, probe_in = refs[:5]
    refs = refs[5:]
    if stepped:
        light_in, refs = refs[0], refs[1:]
    measured_hbm, tile_hbm, refs = refs[0], refs[1], refs[2:]
    if stepped:
        frame, refs = refs[:4], refs[4:]
    rims, refs = refs[:4], refs[4:]
    tile_out, *sides_out, light_out = refs[:10]
    (
        ext,
        new,
        measured_ref,
        probe_now,
        *banks,
        in_sems,
        out_sems,
    ) = refs[10:]
    width = probe_in.shape[1]
    half = width // 2
    rows, cols = tile_hbm.shape[1:]
    edges = margins(half, rows, cols)
    borders = frame_parts(half, rows, cols)
    pairs = [(rim, ext.at[:, at[0], at[1]]) for rim, at in zip(rims, edges)]
    pairs += [
        (measured_hbm.at[:, :, side * half : (side + 1) * half], measured_ref.at[side])
        for side in (0, 1)
    ]
    for whole in (ext, new):
        core = whole.at[:, half : half + rows, half : half + cols]
        if stepped:
            core_rows, core_cols = slice(half, rows - half), slice(half, cols - half)
            pairs += [(part, core.at[:, at[0], at[1]]) for part, at in zip(frame, borders)]
            pairs.append((tile_hbm.at[:, core_rows, core_cols], core.at[:, core_rows, core_cols]))
        else:
            pairs.append((tile_hbm, core))
    loads = [pltpu.make_async_copy(src, dst, in_sems.at[i]) for i, (src, dst) in enumerate(pairs)]
    for load in loads:
        load.start()
    light_out[...] = jnp.zeros_like(light_out)
    for at in edges:
        clear(new, *at)
    probe_ref = probe_now
    if stepped:
        step_probe(rate, probe_in, light_in, probe_now, 8)
    else:
        probe_now[:, 8:, :] = probe_in[...]
    probe_now[:, :8, :] = probe_now[:, width:, :]
    split = 6 + (len(loads) - 6) // 2
    waiting = loads[split:]
    for load in loads[:split]:
        load.wait()
    all_rows = slice(0, rows + width)
    beyond = (edges[0], edges[1], (all_rows, edges[2][1]), (all_rows, edges[3][1]))
    row, col = lax.axis_index("row"), lax.axis_index("col")
    outside = (row == 0, row == mesh_shape[0] - 1, col == 0, col == mesh_shape[1] - 1)
    for i, at in enumerate(beyond):

        @pl.when(outside[i])
        def _():
            clear(ext, *at)

    def dot3(left, right):
        (lh, ll), (rh, rl) = left, right
        return dot(jnp.concatenate([lh, ll, lh], axis=1), jnp.concatenate([rh, rh, rl], axis=0))

    def table(which):
        return table_ref[which, 0], table_ref[which, 1]

    whole = slice(None)
    near, far = slice(0, half), slice(half, width)

    def visit(slot, live, bank, arrived):
        op_high, op_low, res, win, probe_rot, target = (ref.at[bank] for ref in banks)

        def put(which, at_rows, at_cols, value):
            high, low = halves(value)
            op_high[which, at_rows, at_cols] = high
            op_low[which, at_rows, at_cols] = low

        def operand(which):
            return op_high[which], op_low[which]

        row_at = offset_ref[0, slot]
        col_at = offset_ref[1, slot]
        row_base = pl.multiple_of((row_at // 8) * 8, 8)
        col_base = pl.multiple_of((col_at // 128) * 128, 128)
        row_by = row_at - row_base
        col_by = col_at - col_base
        first_lanes = lax.broadcasted_iota(jnp.int32, (CHUNK, half), 1)
        first_rows = lax.broadcasted_iota(jnp.int32, (8, half), 0)
        lane = first_lanes >= col_by
        sub = first_rows >= row_by

        def block(ref, part, first, count, piece):
            at = pl.multiple_of(col_base + piece * 128, 128)
            return ref[part, pl.ds(pl.multiple_of(row_base + first, 8), count), pl.ds(at, 128)]

        for parity, to in enumerate((near, far)):
            picked = pl.ds(parity, half, stride=2)
            for side, span in enumerate((near, far)):
                put(0, to, span, measured_ref[side, slot, picked, :])
        yield
        target[...] = dot(op_high[0], order_ref[...]) + dot(op_low[0], order_ref[...])
        above = (first_rows >= row_by)[None]
        lane_in = first_lanes >= col_by
        for part in (0, 1):
            for first in range(0, width, CHUNK):
                sides = []
                for span in (near, far):
                    block8 = probe_ref[part, first : first + CHUNK + 8, span]
                    block8 = pltpu.roll(block8.reshape(-1, 8, half), row_by, 1)
                    block8 = jnp.where(above, block8[1:], block8[:-1]).reshape(CHUNK, half)
                    sides.append(pltpu.roll(block8, col_by, 1))
                here = slice(first, first + CHUNK)
                probe_rot[part, here, near] = jnp.where(lane_in, sides[0], sides[1])
                probe_rot[part, here, far] = jnp.where(lane_in, sides[1], sides[0])
        yield
        for first in range(0, width, CHUNK):
            here = slice(first, first + CHUNK)
            fields = []
            for part in (0, 1):
                pieces = []
                for piece in range(3):
                    body = block(ext, part, first, CHUNK, piece)
                    if first == 0:
                        tail = block(ext, part, width, 8, piece)
                        body = jnp.concatenate([jnp.where(sub, body[:8], tail), body[8:]], axis=0)
                    pieces.append(body)
                near_cols = jnp.where(lane, pieces[0], pieces[2])
                fields.append((near_cols, pieces[1]))
                win[part, here, near] = near_cols
                win[part, here, far] = pieces[1]
            exits = []
            for side, span in enumerate((near, far)):
                wr, wi = fields[0][side], fields[1][side]
                pr, pi = probe_rot[0, here, span], probe_rot[1, here, span]
                exits.append((pr * wr - pi * wi, pr * wi + pi * wr))
            for part, span in enumerate((near, far)):
                put(0, here, span, exits[0][part] + exits[1][part])
                put(1, here, span, exits[0][part] - exits[1][part])
        yield
        res[0] = dot3(operand(0), table(1))
        res[1] = dot3(operand(1), table(3))
        yield
        for part, rows_to in enumerate((near, far)):
            for parity, cols_to in enumerate((near, far)):
                upper = res[parity, near, rows_to]
                lower = res[parity, far, rows_to]
                put(0, rows_to, cols_to, upper + lower)
                put(1, rows_to, cols_to, upper - lower)
        yield
        res[0] = dot3(table(0), operand(0))
        res[1] = dot3(table(2), operand(1))
        yield
        for parity in (0, 1):
            re, im = res[parity, near, :], res[parity, far, :]
            rows_from = slice(parity * half, (parity + 1) * half)
            misfit = re * re + im * im - target[rows_from, :]
            misfit = jnp.where(live, misfit, 0.0)
            put(parity, near, whole, misfit * re)
            put(parity, far, whole, misfit * im)
        yield
        res[0] = dot3(table(1), operand(0))
        res[1] = dot3(table(3), operand(1))
        yield
        for part, cols_to in enumerate((near, far)):
            for parity, cols_from in enumerate((near, far)):
                first = res[0, cols_to, cols_from]
                second = res[1, cols_to, cols_from]
                put(parity, near, cols_to, first + second)
                put(parity, far, cols_to, first - second)
        yield
        res[0] = dot3(operand(0), table(4))
        res[1] = dot3(operand(1), table(5))
        arrived()
        yield
        for first in range(0, width, CHUNK):
            here = slice(first, first + CHUNK)
            terms = []
            for side, span in enumerate((near, far)):
                er, ei = res[0, here, near], res[0, here, far]
                dr, di = res[1, here, near], res[1, here, far]
                if side == 0:
                    br, bi = er + dr, ei + di
                else:
                    br, bi = er - dr, ei - di
                pr, pi = probe_rot[0, here, span], probe_rot[1, here, span]
                wr, wi = win[0, here, span], win[1, here, span]
                terms.append((pr * br + pi * bi, pr * bi - pi * br))
                light_terms = (wr * br + wi * bi, wr * bi - wi * br)
                for part in (0, 1):
                    win[part, here, span] = light_terms[part]
                    if first == 0:
                        win[part, width : width + 8, span] = light_terms[part][:8]

            def take(part, at, count, piece, value):
                to = pl.ds(pl.multiple_of(col_base + piece * 128, 128), 128)
                span = pl.ds(pl.multiple_of(row_base + at, 8), count)
                new[part, span, to] = new[part, span, to] - value

            for part in (0, 1):
                left_term = terms[0][part]
                right_term = terms[1][part]
                pieces = (
                    jnp.where(lane, left_term, 0.0),
                    right_term,
                    jnp.where(lane, 0.0, left_term),
                )
                for piece, value in enumerate(pieces):
                    if first == 0:
                        take(part, 0, 8, piece, jnp.where(sub, value[:8], 0.0))
                        take(part, 8, CHUNK - 8, piece, value[8:])
                        take(part, width, 8, piece, jnp.where(sub, 0.0, value[:8]))
                    else:
                        take(part, first, CHUNK, piece, value)
        yield
        below = (first_rows < 8 - row_by)[None]
        lane_out = first_lanes < half - col_by
        row_back, col_back = lax.rem(8 - row_by, 8), lax.rem(half - col_by, half)
        for part in (0, 1):
            for first in range(0, width, CHUNK):
                sides = []
                for span in (near, far):
                    block8 = win[part, first : first + CHUNK + 8, span]
                    block8 = pltpu.roll(block8.reshape(-1, 8, half), row_back, 1)
                    block8 = jnp.where(below, block8[:-1], block8[1:]).reshape(CHUNK, half)
                    sides.append(pltpu.roll(block8, col_back, 1))
                turned = (
                    jnp.where(lane_out, sides[0], sides[1]),
                    jnp.where(lane_out, sides[1], sides[0]),
                )
                for i in range(CHUNK // 8):
                    unit = (part * (width // 8) + first // 8 + i) * 2
                    for side in (0, 1):
                        light_out[unit + side] += turned[side][8 * i : 8 * i + 8]

    count = count_ref[0]

    def arrive():
        for load in waiting:
            load.wait()
        waiting.clear()

    def visit_some(group, carry, arrived=lambda: None):
        running = []
        for bank in range(TOGETHER):
            slot = group * TOGETHER + bank
            running.append(visit(jnp.minimum(slot, count - 1), slot < count, bank, arrived))
        step = 0
        while any(running):
            for bank, job in enumerate(running):
                if job is not None and step >= STAGGER * bank:
                    if next(job, "ended") == "ended":
                        running[bank] = None
            step += 1
        return carry

    visit_some(0, 0, arrive)
    lax.fori_loop(1, (count + TOGETHER - 1) // TOGETHER, visit_some, 0)
    core = new.at[:, half : half + rows, half : half + cols]
    pairs = [(new.at[:, at[0], at[1]], out) for at, out in zip(edges, sides_out)]
    pairs += [(core.at[:, at[0], at[1]], out) for at, out in zip(borders, sides_out[4:])]
    inside = (slice(half, rows - half), slice(half, cols - half))
    pairs.append((core.at[:, inside[0], inside[1]], tile_out.at[:, inside[0], inside[1]]))
    stores = [pltpu.make_async_copy(src, dst, out_sems.at[i]) for i, (src, dst) in enumerate(pairs)]
    for store in stores:
        store.start()
    for store in stores:
        store.wait()


def patterns(
    mesh_shape, counts, offsets, tables, order, probe, sums, measured, tile, frame, rims, rate
):
    width = probe.shape[1]
    half = width // 2
    rows, cols = tile.shape[1:]
    ext = (2, rows + width, cols + width)
    flat, tall = (2, half, cols + width), (2, rows, half)
    vmem = pl.BlockSpec(memory_space=pltpu.VMEM)
    smem = pl.BlockSpec(memory_space=pltpu.SMEM)
    hbm = pl.BlockSpec(memory_space=pl.ANY)
    stepped = len(sums) > 0
    units = 2 * width * width // 1024
    inner = (2, half, cols - width)
    outs = [tile.shape, flat, flat, tall, tall, tall, tall, inner, inner, (units, 8, 128)]
    return pl.pallas_call(
        functools.partial(patterns_kernel, mesh_shape, rate, stepped),
        in_specs=[smem] * 2
        + [vmem] * (3 + len(sums))
        + [hbm, pl.BlockSpec(memory_space=pltpu.HBM)]
        + [hbm] * (4 + len(frame)),
        out_specs=[pl.BlockSpec(memory_space=pltpu.HBM)] + [hbm] * 8 + [vmem],
        out_shape=[jax.ShapeDtypeStruct(shape, F32) for shape in outs],
        scratch_shapes=[
            pltpu.VMEM(ext, F32),
            pltpu.VMEM(ext, F32),
            pltpu.VMEM((2, measured.shape[0], width, half), F32),
            pltpu.VMEM((2, width + 8, width), F32),
            pltpu.VMEM((TOGETHER,) + probe.shape, BF16),
            pltpu.VMEM((TOGETHER,) + probe.shape, BF16),
            pltpu.VMEM((TOGETHER,) + probe.shape, F32),
            pltpu.VMEM((TOGETHER, 2, width + 8, width), F32),
            pltpu.VMEM((TOGETHER,) + probe.shape, F32),
            pltpu.VMEM((TOGETHER, width, width), F32),
            pltpu.SemaphoreType.DMA((16,)),
            pltpu.SemaphoreType.DMA((9,)),
        ],
        compiler_params=pltpu.CompilerParams(vmem_limit_bytes=(35 if stepped else 35) * MIB),
        name="patterns",
    )(counts, offsets, tables, order, probe, *sums, measured, tile, *frame, *rims)


MIDDLES = 4
LAST_STEPS = ("sum", "m0", "sum", "rows", "m1", "sum", "m2", "frame", "sum", "take_rows", "m3", "sum", "t0", "t1", "sum", "t2", "t3", "take_ends")
AGAIN_STEPS = ("sum", "rows", "m0", "m1", "m2", "sum", "m3", "frame", "sum", "take_rows", "t0", "sum", "t1", "take_ends", "sum", "t2", "corners", "sum", "t3")


def when(condition, act):
    if condition is None:
        act()
    else:
        pl.when(condition)(act)


class Exchange:
    def __init__(self, place, send_sems, recv_sems):
        self.place = place
        self.sems = (send_sems, recv_sems)
        self.used = 0
        self.open = []

    def send(self, src, dst, to, landing=None, also=None):
        at = self.used
        self.used += 1
        go, come = self.place.gates(to, also)
        copy = self.describe(src, dst, to, at)
        when(go, copy.start)
        arrival = copy if landing is None else self.describe(src, landing, to, at)
        self.open.append((go, copy.wait_send))
        return lambda: when(come, arrival.wait_recv)

    def describe(self, src, dst, to, at):
        return pltpu.make_async_remote_copy(
            src_ref=src,
            dst_ref=dst,
            send_sem=self.sems[0].at[at],
            recv_sem=self.sems[1].at[at],
            device_id=to,
            device_id_type=MESH,
        )

    def finish(self):
        for go, wait_send in self.open:
            when(go, wait_send)


def greet(peers):
    barrier = pltpu.get_barrier_semaphore()
    for peer in peers:
        pl.semaphore_signal(barrier, inc=1, device_id=peer, device_id_type=MESH)
    pl.semaphore_wait(barrier, len(peers))


class Place:
    def __init__(self, mesh_shape):
        self.n_row, self.n_col = mesh_shape
        self.row = lax.axis_index("row")
        self.col = lax.axis_index("col")
        self.up = (lax.rem(self.row + self.n_row - 1, self.n_row), self.col)
        self.down = (lax.rem(self.row + 1, self.n_row), self.col)
        self.left = (self.row, lax.rem(self.col + self.n_col - 1, self.n_col))
        self.right = (self.row, lax.rem(self.col + 1, self.n_col))

    def gates(self, to, also):
        if to is self.up or to is self.down:
            pair = (self.row > 0, self.row < self.n_row - 1)
        elif to is self.left or to is self.right:
            pair = (self.col > 0, self.col < self.n_col - 1)
        else:
            return None, None
        if also is not None:
            pair = tuple(jnp.logical_and(one, also) for one in pair)
        return pair if to is self.up or to is self.left else pair[::-1]

    def near(self):
        return [self.up, self.down, self.left, self.right]

    def reducers(self):
        core = lax.rem(self.row, 2)
        partner = (self.row + 1 - 2 * core, self.col)
        along = [
            (lax.rem(self.row + 2 * j, self.n_row), self.col) for j in range(1, self.n_row // 2)
        ]
        across = [(self.row, lax.rem(self.col + j, self.n_col)) for j in range(1, self.n_col)]
        return partner, along, across


def probe_sum(place, net, light, total, first, second, got_core, got_row, got_col):
    partner, along, across = place.reducers()
    core, x = lax.rem(place.row, 2), lax.div(place.row, 2)
    n_x, n_col = place.n_row // 2, place.n_col
    big, mid = first.shape[0], second.shape[0]
    arrive = net.send(light.at[pl.ds((1 - core) * big, big)], got_core, partner)
    yield
    arrive()

    @pl.loop(0, big)
    def _(i):
        first[i] = light[core * big + i] + got_core[i]

    waits = []
    for j, peer in enumerate(along):
        there = lax.div(peer[0], 2)
        waits.append(net.send(first.at[pl.ds(there * mid, mid)], got_row.at[j], peer))
    yield
    for wait in waits:
        wait()

    @pl.loop(0, mid)
    def _(i):
        value = first[x * mid + i]
        for j in range(n_x - 1):
            value = value + got_row[j, i]
        second[i] = value

    waits = [net.send(second.at[peer[1]], got_col.at[j], peer) for j, peer in enumerate(across)]
    yield
    for wait in waits:
        wait()
    value = second[place.col]
    for j in range(n_col - 1):
        value = value + got_col[j]
    corner = core * big + x * mid
    mine = corner + place.col
    total[mine] = value
    waits = []
    for j, peer in enumerate(across):
        source = lax.rem(place.col + n_col - (j + 1), n_col)
        waits.append(net.send(total.at[mine], total.at[mine], peer, total.at[corner + source]))
    yield
    for wait in waits:
        wait()
    block = pl.ds(corner, mid)
    waits = []
    for j, peer in enumerate(along):
        source = lax.rem(x + n_x - (j + 1), n_x)
        landing = total.at[pl.ds(core * big + source * mid, mid)]
        waits.append(net.send(total.at[block], total.at[block], peer, landing))
    yield
    for wait in waits:
        wait()
    block = pl.ds(core * big, big)
    landing = total.at[pl.ds((1 - core) * big, big)]
    arrive = net.send(total.at[block], total.at[block], partner, landing)
    yield
    arrive()


def fetch_kernel(mesh_shape, half, tile, top, bottom, left, right, send_sems, recv_sems):
    place = Place(mesh_shape)
    net = Exchange(place, send_sems, recv_sems)
    rows, cols = tile.shape[1:]
    greet(place.near())
    ends = (slice(0, half), slice(rows - half, rows))
    first, last = slice(0, half), slice(cols - half, cols)
    inner = slice(half, half + cols)
    waits = []
    for end in ends:
        waits.append(net.send(tile.at[:, end, first], right.at[:, end], place.left))
        waits.append(net.send(tile.at[:, end, last], left.at[:, end], place.right))
    later = [
        net.send(tile.at[:, ends[0]], bottom.at[:, :, inner], place.up),
        net.send(tile.at[:, ends[1]], top.at[:, :, inner], place.down),
    ]
    middle = slice(half, rows - half)
    later.append(net.send(tile.at[:, middle, first], right.at[:, middle], place.left))
    later.append(net.send(tile.at[:, middle, last], left.at[:, middle], place.right))
    for wait in waits:
        wait()
    outer = (slice(0, half), slice(half + cols, 2 * half + cols))
    there = (place.col > 0, place.col < place.n_col - 1)
    for rim, to, also in zip((left, right), outer, there):
        later.append(net.send(rim.at[:, ends[0]], bottom.at[:, :, to], place.up, None, also))
        later.append(net.send(rim.at[:, ends[1]], top.at[:, :, to], place.down, None, also))
    for wait in later:
        wait()
    net.finish()


def fetch_rims(mesh_shape, tile, half):
    rows, cols = tile.shape[1:]
    flat = jax.ShapeDtypeStruct((2, half, cols + 2 * half), F32)
    tall = jax.ShapeDtypeStruct((2, rows, half), F32)
    hbm = pl.BlockSpec(memory_space=pl.ANY)
    return pl.pallas_call(
        functools.partial(fetch_kernel, mesh_shape, half),
        in_specs=[pl.BlockSpec(memory_space=pltpu.HBM)],
        out_specs=[hbm] * 4,
        out_shape=[flat, flat, tall, tall],
        scratch_shapes=[pltpu.SemaphoreType.DMA((12,)), pltpu.SemaphoreType.DMA((12,))],
        compiler_params=pltpu.CompilerParams(
            collective_id=1, has_side_effects=True, vmem_limit_bytes=49 * MIB
        ),
        name="fetch_rims",
    )(tile)


def add_rows(target, at_rows, source, from_rows, from_cols):
    step = 32

    @pl.loop(0, at_rows.stop - at_rows.start, step=step)
    def _(i):
        to = pl.ds(pl.multiple_of(at_rows.start + i, step), step)
        here = pl.ds(pl.multiple_of(from_rows.start + i, step), step)
        target[:, to, :] = target[:, to, :] + source[:, here, from_cols]


def settle_kernel(mesh_shape, half, again, *refs):
    grad_top, grad_bottom, grad_left, grad_right, *border, light = refs[:9]
    refs = refs[9:]
    out_left, out_right, out_top, out_bottom, total_out = refs[:5]
    refs = refs[5:]
    if again:
        top, bottom, left, right = refs[:4]
        refs = refs[4:]
    (
        own_left,
        own_right,
        own_top,
        own_bottom,
        end_left,
        end_right,
        got_top,
        got_bottom,
        got_left,
        got_right,
        total,
        first_sum,
        second_sum,
        got_core,
        got_row,
        got_col,
        load_sems,
        send_sems,
        recv_sems,
    ) = refs
    place = Place(mesh_shape)
    net = Exchange(place, send_sems, recv_sems)
    rows, cols = grad_left.shape[1], grad_top.shape[2] - 2 * half
    partner, along, across = place.reducers()
    further = (lax.rem(place.row + place.n_row - 1 + 2 * lax.rem(place.row, 2), place.n_row), place.col)
    greet([partner, further] + along + across)

    up_end, down_end = slice(0, half), slice(rows - half, rows)
    whole = slice(0, half)
    wide = (slice(0, half), slice(half, 2 * half), slice(2 * half, cols), slice(cols, cols + half))
    wide = wide + (slice(cols + half, cols + 2 * half),)
    bounds = [half + i * (rows - 2 * half) // MIDDLES for i in range(MIDDLES + 1)]
    middles = [slice(i, j) for i, j in zip(bounds, bounds[1:])]
    pairs = (
        (grad_left.at[:, up_end], end_left.at[0]),
        (grad_left.at[:, down_end], end_left.at[1]),
        (grad_right.at[:, up_end], end_right.at[0]),
        (grad_right.at[:, down_end], end_right.at[1]),
    ) + tuple(zip(border, (own_left, own_right, own_top, own_bottom)))
    loads = [pltpu.make_async_copy(src, dst, load_sems.at[i]) for i, (src, dst) in enumerate(pairs)]
    for load in loads:
        load.start()
    sums = probe_sum(place, net, light, total, first_sum, second_sum, got_core, got_row, got_col)
    waits = {}

    def send_rows():
        waits["rows"] = [
            net.send(grad_top, got_bottom, place.up),
            net.send(grad_bottom, got_top, place.down),
        ]

    def send_middle(span):
        waits[span.start] = [
            net.send(grad_left.at[:, span], got_right.at[:, span], place.left),
            net.send(grad_right.at[:, span], got_left.at[:, span], place.right),
        ]

    def take_rows():
        for wait in waits["rows"]:
            wait()
        for end, (got, own, span, inside) in enumerate(
            (
                (got_top, own_top, up_end, place.row > 0),
                (got_bottom, own_bottom, down_end, place.row < place.n_row - 1),
            )
        ):

            @pl.when(inside)
            def _():
                add_rows(end_left.at[end], whole, got, whole, wide[0])
                add_rows(own_left, span, got, whole, wide[1])
                add_rows(own, whole, got, whole, wide[2])
                add_rows(own_right, span, got, whole, wide[3])
                add_rows(end_right.at[end], whole, got, whole, wide[4])

        waits["ends"] = []
        for end, span in enumerate((up_end, down_end)):
            waits["ends"].append(net.send(end_left.at[end], got_right.at[:, span], place.left))
            waits["ends"].append(net.send(end_right.at[end], got_left.at[:, span], place.right))

    def take_cols(span):
        @pl.when(place.col > 0)
        def _():
            add_rows(own_left, span, got_left, span, slice(None))

        @pl.when(place.col < place.n_col - 1)
        def _():
            add_rows(own_right, span, got_right, span, slice(None))

    def give_cols(span):
        return [
            net.send(own_left.at[:, span], right.at[:, span], place.left),
            net.send(own_right.at[:, span], left.at[:, span], place.right),
        ]

    later = []

    def take_middle(span):
        for wait in waits[span.start]:
            wait()
        take_cols(span)
        if again:
            later.extend(give_cols(span))

    def take_ends():
        for wait in waits["ends"]:
            wait()
        take_cols(up_end)
        take_cols(down_end)
        if again:
            waits["corners"] = give_cols(up_end) + give_cols(down_end)
            for span, own, rim, to in (
                (up_end, own_top, bottom, place.up),
                (down_end, own_bottom, top, place.down),
            ):
                later.append(net.send(own_left.at[:, span], rim.at[:, :, wide[1]], to))
                later.append(net.send(own, rim.at[:, :, wide[2]], to))
                later.append(net.send(own_right.at[:, span], rim.at[:, :, wide[3]], to))

    def send_corners():
        if again:
            for wait in waits["corners"]:
                wait()
            there = (place.col > 0, place.col < place.n_col - 1)
            for rim, to, also in zip((left, right), (wide[0], wide[4]), there):
                above, below = bottom.at[:, :, to], top.at[:, :, to]
                later.append(net.send(rim.at[:, up_end], above, place.up, None, also))
                later.append(net.send(rim.at[:, down_end], below, place.down, None, also))

    def load_frame():
        for load in loads:
            load.wait()

    plain = {
        "rows": send_rows,
        "take_rows": take_rows,
        "take_ends": take_ends,
        "corners": send_corners,
        "frame": load_frame,
        "sum": lambda: next(sums, None),
    }
    for step in AGAIN_STEPS if again else LAST_STEPS:
        if step in plain:
            plain[step]()
        elif step[0] == "m":
            send_middle(middles[int(step[1:])])
        else:
            take_middle(middles[int(step[1:])])
    for _ in sums:
        pass
    stores = [
        pltpu.make_async_copy(src, dst, load_sems.at[i])
        for i, (src, dst) in enumerate(
            (
                (own_left, out_left),
                (own_right, out_right),
                (own_top, out_top),
                (own_bottom, out_bottom),
                (total, total_out),
            )
        )
    ]
    for store in stores:
        store.start()
    for wait in later:
        wait()
    net.finish()
    for store in stores:
        store.wait()


def settle(mesh_shape, strips, border, light, again):
    rows, half = strips[2].shape[1:]
    cols = strips[0].shape[2] - 2 * half
    n_row, n_col = mesh_shape
    big, mid = light.shape[0] // 2, light.shape[0] // n_row
    unit = light.shape[1:]
    flat, tall = (2, half, cols + 2 * half), (2, rows, half)
    inner, ends = (2, half, cols - 2 * half), (2, 2, half, half)
    outs = [tall, tall, inner, inner, light.shape] + ([flat, flat, tall, tall] if again else [])
    copies = 8 + 2 * MIDDLES + 2 * (n_col - 1) + 2 * (n_row // 2 - 1) + again * (14 + 2 * MIDDLES)
    hbm = pl.BlockSpec(memory_space=pl.ANY)
    vmem = pl.BlockSpec(memory_space=pltpu.VMEM)
    return pl.pallas_call(
        functools.partial(settle_kernel, mesh_shape, half, again),
        in_specs=[hbm] * 8 + [vmem],
        out_specs=[hbm] * len(outs),
        out_shape=[jax.ShapeDtypeStruct(shape, F32) for shape in outs],
        scratch_shapes=[
            pltpu.VMEM(tall, F32),
            pltpu.VMEM(tall, F32),
            pltpu.VMEM(inner, F32),
            pltpu.VMEM(inner, F32),
            pltpu.VMEM(ends, F32),
            pltpu.VMEM(ends, F32),
            pltpu.VMEM(flat, F32),
            pltpu.VMEM(flat, F32),
            pltpu.VMEM(tall, F32),
            pltpu.VMEM(tall, F32),
            pltpu.VMEM(light.shape, F32),
            pltpu.VMEM((big,) + unit, F32),
            pltpu.VMEM((mid,) + unit, F32),
            pltpu.VMEM((big,) + unit, F32),
            pltpu.VMEM((n_row // 2 - 1, mid) + unit, F32),
            pltpu.VMEM((n_col - 1,) + unit, F32),
            pltpu.SemaphoreType.DMA((8,)),
            pltpu.SemaphoreType.DMA((copies,)),
            pltpu.SemaphoreType.DMA((copies,)),
        ],
        compiler_params=pltpu.CompilerParams(
            collective_id=2 if again else 3, has_side_effects=True, vmem_limit_bytes=20 * MIB
        ),
        name="settle_and_fetch" if again else "settle",
    )(*strips, *border, light)


def finish_kernel(rate, *refs):
    probe, sum_first, sum_last, left, right, top, bottom, tile_in, tile, probe_out, sems = refs
    rows, cols = tile.shape[1:]
    half = left.shape[2]
    first, last, core_cols = slice(0, half), slice(cols - half, cols), slice(half, cols - half)
    pairs = (
        (left, tile.at[:, :, first]),
        (right, tile.at[:, :, last]),
        (top, tile.at[:, :half, core_cols]),
        (bottom, tile.at[:, rows - half :, core_cols]),
    )
    stores = [pltpu.make_async_copy(src, dst, sems.at[i]) for i, (src, dst) in enumerate(pairs)]
    for store in stores:
        store.start()
    step_probe(rate, probe, sum_first, probe_out)
    step_probe(rate, probe_out, sum_last, probe_out)
    for store in stores:
        store.wait()


def finish(probe, sums, frame, tile, rate):
    hbm = pl.BlockSpec(memory_space=pl.ANY)
    vmem = pl.BlockSpec(memory_space=pltpu.VMEM)
    return pl.pallas_call(
        functools.partial(finish_kernel, rate),
        in_specs=[vmem] * 7 + [hbm],
        out_specs=[hbm, vmem],
        out_shape=[
            jax.ShapeDtypeStruct(tile.shape, F32),
            jax.ShapeDtypeStruct(probe.shape, F32),
        ],
        scratch_shapes=[pltpu.SemaphoreType.DMA((4,))],
        input_output_aliases={7: 0},
        compiler_params=pltpu.CompilerParams(vmem_limit_bytes=40 * MIB),
        name="finish",
    )(probe, *sums, *frame, tile)


def step_probe(rate, probe, light, out, shift=0):
    width = probe.shape[1]
    per_part = width // 8
    for part in (0, 1):

        @pl.loop(0, per_part)
        def _(i):
            span = pl.ds(pl.multiple_of(i * 8, 8), 8)
            for side in (0, 1):
                lanes = slice(side * 128, (side + 1) * 128)
                block = light[(part * per_part + i) * 2 + side]
                to = pl.ds(pl.multiple_of(i * 8 + shift, 8), 8)
                out[part, to, lanes] = probe[part, span, lanes] - rate * block


def per_device(mesh_shape, object_field, illumination, measured, offsets, counts):
    width = illumination.shape[1]
    half = width // 2
    total = measured.shape[0] * mesh_shape[0] * mesh_shape[1]
    rate = LIGHT_RATE / total / OBJECT_RATE
    tables = jnp.asarray(factor_tables(width))
    order = jnp.asarray(parity_order(width))
    sums = []
    tile, frame, probe = object_field, (), illumination
    rims = fetch_rims(mesh_shape, tile, half)
    for sweep in range(ITERS):
        tile, *sides, light = patterns(
            mesh_shape, counts, offsets.T, tables, order, probe, sums, measured, tile, frame, rims, rate
        )
        found = settle(mesh_shape, sides[:4], sides[4:], light, sweep < ITERS - 1)
        frame, rims = found[:4], found[5:]
        sums.append(found[4])
    return finish(probe, sums, frame, tile, rate)


def solution(mesh):
    placed = (
        P(None, "row", "col"),
        P(),
        P(("row", "col"), None, None),
        P(("row", "col"), None),
        P(("row", "col")),
    )
    mesh_shape = (mesh.shape["row"], mesh.shape["col"])
    return jax.shard_map(
        functools.partial(per_device, mesh_shape),
        mesh=mesh,
        in_specs=placed,
        out_specs=(P(None, "row", "col"), P()),
        check_vma=False,
    )
```
